32 devices in a mesh: species: 2 (over core), dp: 4 (over z), seq: 4 (over y, x).
Axes of the slice: x: 2, y: 2, z: 4, core: 2. Of those that a mesh axis runs over, the one named last changes fastest.
Arguments:
- inputs: bfloat16 [2, 4, 1536, 1536], P('species', 'dp', 'seq'), may hold values from -30 to 30
- crop_start: int32 [2, 4], P('species', 'dp'), may hold values from 96 to 544, as said below
- rel_bucket: int32 [3071], replicated, may hold values from 0 to 31
- conv_weight: bfloat16 [7680, 1536], P(('species', 'dp', 'seq')), may hold values from -0.125 to 0.125
- query_weight: bfloat16 [1536, 512], P(('species', 'dp', 'seq')), may hold values from -0.15625 to 0.15625
- key_weight: bfloat16 [1536, 512], P(('species', 'dp', 'seq')), may hold values from -0.15625 to 0.15625
- value_weight: bfloat16 [1536, 1536], P(('species', 'dp', 'seq')), may hold values from -0.15625 to 0.15625
- out_weight: bfloat16 [1536, 1536], P(('species', 'dp', 'seq')), may hold values from -2 to 2
- up_weight: bfloat16 [1536, 3072], P(('species', 'dp', 'seq')), may hold values from -0.15625 to 0.15625
- down_weight: bfloat16 [3072, 1536], P(('species', 'dp', 'seq')), may hold values from -0.109375 to 0.109375
- point_weight: bfloat16 [1536, 3072], P(('species', 'dp', 'seq')), may hold values from -0.15625 to 0.15625
- rel_table: bfloat16 [256], P(('species', 'dp', 'seq')), may hold values from -3 to 3
- bn_gain: bfloat16 [1536], P(('species', 'dp', 'seq')), may hold values from 0.5 to 1.5
- bn_shift: bfloat16 [1536], P(('species', 'dp', 'seq')), may hold values from -1 to 1
- conv_bias: bfloat16 [1536], P(('species', 'dp', 'seq')), may hold values from -1 to 1
- attn_gain: bfloat16 [1536], P(('species', 'dp', 'seq')), may hold values from 0.5 to 1.5
- attn_shift: bfloat16 [1536], P(('species', 'dp', 'seq')), may hold values from -1 to 1
- ffn_gain: bfloat16 [1536], P(('species', 'dp', 'seq')), may hold values from 0.5 to 1.5
- ffn_shift: bfloat16 [1536], P(('species', 'dp', 'seq')), may hold values from -1 to 1
- up_bias: bfloat16 [3072], P(('species', 'dp', 'seq')), may hold values from -1 to 1
- down_bias: bfloat16 [1536], P(('species', 'dp', 'seq')), may hold values from -1 to 1
- point_bias: bfloat16 [3072], P(('species', 'dp', 'seq')), may hold values from -1 to 1
- head_weight: bfloat16 [2, 3072, 5313], P('species', ('dp', 'seq')), may hold values from -0.109375 to 0.109375
- pred_grad: bfloat16 [2, 4, 896, 5313], P('species', 'dp', 'seq'), may hold values from -6 to 6
Outputs:
- predictions: bfloat16 [2, 4, 896, 5313], P('species', 'dp', 'seq')
- input_grad: float32 [2, 4, 1536, 1536], P('species', 'dp', 'seq')
- conv_weight_grad: float32 [7680, 1536], P(('species', 'dp', 'seq'))
- query_weight_grad: float32 [1536, 512], P(('species', 'dp', 'seq'))
- key_weight_grad: float32 [1536, 512], P(('species', 'dp', 'seq'))
- value_weight_grad: float32 [1536, 1536], P(('species', 'dp', 'seq'))
- out_weight_grad: float32 [1536, 1536], P(('species', 'dp', 'seq'))
- up_weight_grad: float32 [1536, 3072], P(('species', 'dp', 'seq'))
- down_weight_grad: float32 [3072, 1536], P(('species', 'dp', 'seq'))
- point_weight_grad: float32 [1536, 3072], P(('species', 'dp', 'seq'))
- rel_table_grad: float32 [256], P(('species', 'dp', 'seq'))
- bn_gain_grad: float32 [1536], P(('species', 'dp', 'seq'))
- bn_shift_grad: float32 [1536], P(('species', 'dp', 'seq'))
- conv_bias_grad: float32 [1536], P(('species', 'dp', 'seq'))
- attn_gain_grad: float32 [1536], P(('species', 'dp', 'seq'))
- attn_shift_grad: float32 [1536], P(('species', 'dp', 'seq'))
- ffn_gain_grad: float32 [1536], P(('species', 'dp', 'seq'))
- ffn_shift_grad: float32 [1536], P(('species', 'dp', 'seq'))
- up_bias_grad: float32 [3072], P(('species', 'dp', 'seq'))
- down_bias_grad: float32 [1536], P(('species', 'dp', 'seq'))
- point_bias_grad: float32 [3072], P(('species', 'dp', 'seq'))
- head_weight_grad: float32 [2, 3072, 5313], P('species', ('dp', 'seq'))
The draws below stay inside these ranges and needn't reach their ends.
Inputs may be any that keep to these rules, and one draw needn't show every extreme that they name: `crop_start`: the crop of 896 bins lies inside its sequence; in each species one sequence starts at the least value and another at the most. `rel_bucket`: entry j - i + 1535 holds the bucket of relative distance j - i.
All inputs are finite; a program needn't handle non-finite values.
Results may differ from the reference program's by a relative error of at most 0.038.
Values may be sent and summed in bfloat16 or wider, within the bound.
No kernel may reach another device: no remote copies, remote signals or barrier semaphores. Data moves between devices by JAX's collectives and lax.ppermute only.
A program may use at most 448 MiB of HBM per device.

```python
import jax
import jax.numpy as jnp
from jax import lax

C = 1536
HEADS = 8
QK = 64
V = 192
FF = 3072
HID = 3072
TRK = 5313
TRK_M = 1643
WIDTH = 5
NB = 32
LEN = 1536
CROP = 896
GSEQ = 4
BINS_DEV = 384
CROP_DEV = 224


def draw_inputs(key, part):
    key = jax.random.fold_in(key, 11)
    base_key, rough_key, column_key = jax.random.split(key, 3)
    shape = (2, GSEQ, LEN, C)
    base = jnp.clip(jax.random.normal(base_key, shape, jnp.float32), -4.0, 4.0)
    column = jnp.exp(jax.random.uniform(column_key, (C,), jnp.float32, jnp.log(0.4), jnp.log(2.5)))
    order = (jnp.arange(2 * GSEQ, dtype=jnp.float32)[:, None] * LEN + jnp.arange(LEN, dtype=jnp.float32)[None, :]) / (2.0 * GSEQ * LEN - 1.0)
    rising = jnp.exp(order * jnp.log(3.0)).reshape(2, GSEQ, LEN, 1)
    rough = jnp.exp(jax.random.uniform(rough_key, (2, GSEQ, LEN, 1), jnp.float32, 0.0, jnp.log(3.0)))
    return (base * rising * rough * column / 3.0).astype(jnp.bfloat16)


def draw_crop_start(key, part):
    key = jax.random.fold_in(key, 5)
    base_key, order_key = jax.random.split(key, 2)
    shards = LEN // BINS_DEV
    least = max(0, (shards - 1) * (BINS_DEV - CROP_DEV) - BINS_DEV)
    most = min(2 * BINS_DEV - CROP_DEV, LEN - CROP)
    base = jax.random.randint(base_key, (2, GSEQ), least, most + 1, dtype=jnp.int32)
    orders = jax.vmap(lambda k: jax.random.permutation(k, GSEQ))(jax.random.split(order_key, 2))
    places = jnp.arange(GSEQ, dtype=jnp.int32)[None, :]
    base = jnp.where(places == orders[:, 0:1], least, base)
    base = jnp.where(places == orders[:, 1:2], most, base)
    return base.astype(jnp.int32)


def with_ends(drawn, stream_key, low, high):
    spot = [jax.random.randint(jax.random.fold_in(stream_key, axis), (), 0, length) for axis, length in enumerate(drawn.shape)]
    main_axis = drawn.shape.index(max(drawn.shape))
    neighbour = spot[:main_axis] + [(spot[main_axis] + 1) % drawn.shape[main_axis]] + spot[main_axis + 1:]
    return drawn.at[tuple(spot)].set(low).at[tuple(neighbour)].set(high)


def block_scale(own_key, shape, cuts, low, largest):
    level = 1.0
    for axis_at, shards_of in cuts:
        heights = jax.random.uniform(jax.random.fold_in(jax.random.fold_in(own_key, 6), axis_at), (shards_of,), jnp.float32, low / len(cuts), largest / len(cuts))
        level = level * jnp.repeat(jnp.exp(heights), shape[axis_at] // shards_of).reshape((-1,) + (1,) * (len(shape) - 1 - axis_at))
    return level


def scatter_about(key, shape, scale, bound, cuts=(), held_as=jnp.bfloat16):
    result = scale * jax.random.normal(key, shape, jnp.float32)
    if cuts:
        result = result * block_scale(key, shape, cuts, -0.22, 0.18)
    return jnp.clip(result, -bound, bound).astype(held_as)


def setup_inputs(seed: int = 0) -> dict:
    streams_of = jax.random.split(jax.random.key(seed), 25)
    inputs = draw_inputs(jax.random.fold_in(streams_of[24], 71), 0)
    crop_start = draw_crop_start(jax.random.fold_in(streams_of[24], 71), 0)
    rel_bucket = with_ends(jax.random.randint(streams_of[2], (2 * LEN - 1,), 0, NB), jax.random.fold_in(streams_of[2], 1), 0, NB - 1).astype(jnp.int32)
    conv_weight = scatter_about(streams_of[3], (WIDTH * C, C), (WIDTH * C // 4) ** -0.5, 0.125, ((0, 32),))
    query_weight = scatter_about(streams_of[4], (C, HEADS * QK), C ** -0.5, 0.15625, ((0, 32),))
    key_weight = scatter_about(streams_of[5], (C, HEADS * QK), C ** -0.5, 0.15625, ((0, 32),))
    value_weight = scatter_about(streams_of[6], (C, C), C ** -0.5, 0.15625, ((0, 32),))
    out_weight = scatter_about(streams_of[7], (C, C), (C * 8 // LEN) ** -0.5, 2.0, ((0, 32),))
    up_weight = scatter_about(streams_of[8], (C, FF), C ** -0.5, 0.15625, ((0, 32),))
    down_weight = scatter_about(streams_of[9], (FF, C), FF ** -0.5, 0.109375, ((0, 32),))
    point_weight = scatter_about(streams_of[10], (C, HID), C ** -0.5, 0.15625, ((0, 32),))
    rel_table = scatter_about(streams_of[11], (HEADS * NB,), 1.0, 3.0, ((0, 32),))
    bn_gain = jnp.clip(1.0 + 0.1 * jax.random.normal(streams_of[12], (C,), jnp.float32), 0.5, 1.5).astype(jnp.bfloat16)
    bn_shift = scatter_about(streams_of[13], (C,), 0.3, 1.0, ((0, 32),))
    conv_bias = scatter_about(streams_of[14], (C,), 0.3, 1.0, ((0, 32),))
    attn_gain = jnp.clip(1.0 + 0.1 * jax.random.normal(streams_of[15], (C,), jnp.float32), 0.5, 1.5).astype(jnp.bfloat16)
    attn_shift = scatter_about(streams_of[16], (C,), 0.3, 1.0, ((0, 32),))
    ffn_gain = jnp.clip(1.0 + 0.1 * jax.random.normal(streams_of[17], (C,), jnp.float32), 0.5, 1.5).astype(jnp.bfloat16)
    ffn_shift = scatter_about(streams_of[18], (C,), 0.3, 1.0, ((0, 32),))
    up_bias = scatter_about(streams_of[19], (FF,), 0.3, 1.0, ((0, 32),))
    down_bias = scatter_about(streams_of[20], (C,), 0.3, 1.0, ((0, 32),))
    point_bias = scatter_about(streams_of[21], (HID,), 0.3, 1.0, ((0, 32),))
    head_weight = scatter_about(streams_of[22], (2, HID, TRK), HID ** -0.5, 0.109375, ((0, 2), (1, 16)))
    pred_grad = scatter_about(streams_of[23], (2, GSEQ, CROP, TRK), 1.0, 6.0, ((0, 2), (1, 4), (2, 4)))
    return dict(inputs=inputs, crop_start=crop_start, rel_bucket=rel_bucket, conv_weight=conv_weight, query_weight=query_weight, key_weight=key_weight, value_weight=value_weight, out_weight=out_weight, up_weight=up_weight, down_weight=down_weight, point_weight=point_weight, rel_table=rel_table, bn_gain=bn_gain, bn_shift=bn_shift, conv_bias=conv_bias, attn_gain=attn_gain, attn_shift=attn_shift, ffn_gain=ffn_gain, ffn_shift=ffn_shift, up_bias=up_bias, down_bias=down_bias, point_bias=point_bias, head_weight=head_weight, pred_grad=pred_grad)


@jax.custom_vjp
def low(v):
    return lax.optimization_barrier(v.astype(jnp.bfloat16)).astype(jnp.float32)

@jax.custom_vjp
def low_back(v):
    return v

def low_keep(v):
    return (low(v), None)

def low_pass(kept, grad):
    return (grad,)

def back_keep(v):
    return (v, None)

def back_low(kept, grad):
    return (low(grad),)
low.defvjp(low_keep, low_pass)
low_back.defvjp(back_keep, back_low)
EPSILON = 1e-05
HIGHEST = lax.Precision.HIGHEST

def matmul(left, right):
    return jnp.matmul(left, right, precision=HIGHEST)

def layer_norm(value_entries, gain, shift):
    centre = lax.optimization_barrier(jnp.mean(value_entries, axis=-1, keepdims=True))
    centred = value_entries - centre
    spread = lax.optimization_barrier(jnp.mean(centred * centred, axis=-1, keepdims=True))
    return centred * lax.rsqrt(spread + EPSILON) * gain + shift

def sequence_forward(params, rel_bucket, seq_inputs, species_id, offset, channel_average, inverse_deviation):
    conv_weight, query_weight, key_weight, value_weight, out_weight, up_weight, down_weight, point_weight, rel_table, bn_gain, bn_shift, conv_bias, attn_gain, attn_shift, ffn_gain, ffn_shift, up_bias, down_bias, point_bias, head_weight = params
    normed_rows = (seq_inputs - channel_average) * inverse_deviation * bn_gain + bn_shift
    activity = low(jax.nn.gelu(normed_rows))
    half_width = WIDTH // 2
    padded = jnp.pad(activity, ((half_width, half_width), (0, 0)))
    kernel = conv_weight.reshape(WIDTH, C, C)
    conv_out = conv_bias + jnp.zeros((LEN, C), jnp.float32)
    for tap_index in range(WIDTH):
        conv_out = conv_out + matmul(padded[tap_index:tap_index + LEN], kernel[tap_index])
    conv_out = low_back(conv_out)
    first_sum = seq_inputs + conv_out
    normed_one = low(layer_norm(first_sum, attn_gain, attn_shift))
    queries = low_back(low(matmul(normed_one, query_weight))).reshape(LEN, HEADS, QK)
    key_rows = low_back(low(matmul(normed_one, key_weight))).reshape(LEN, HEADS, QK)
    value_rows = low_back(low(matmul(normed_one, value_weight))).reshape(LEN, HEADS, V)
    positions = jnp.arange(LEN)
    distance = positions[None, :] - positions[:, None] + LEN - 1
    table = rel_table.reshape(HEADS, NB)
    dist_bias = table[:, rel_bucket]
    scores = jnp.einsum('ihd,jhd->hij', queries, key_rows, precision=HIGHEST) * QK ** (-0.5)
    scores = low_back(scores + dist_bias[:, distance])
    row_max = lax.optimization_barrier(jnp.max(scores, axis=-1, keepdims=True))
    exp_scores = jnp.exp(scores - row_max)
    attn_prob = low(exp_scores / lax.optimization_barrier(jnp.sum(exp_scores, axis=-1, keepdims=True)))
    mixed = jnp.einsum('hij,jhd->ihd', attn_prob, value_rows, precision=HIGHEST).reshape(LEN, HEADS * V)
    mixed = low_back(low(mixed))
    second_sum = first_sum + low_back(matmul(mixed, out_weight))
    normed_two = low(layer_norm(second_sum, ffn_gain, ffn_shift))
    up_pre = low_back(matmul(normed_two, up_weight) + up_bias)
    up_act = low(jax.nn.gelu(up_pre))
    third_sum = second_sum + low_back(matmul(up_act, down_weight) + down_bias)
    cropped = low_back(low(lax.dynamic_slice_in_dim(third_sum, offset, CROP, 0)))
    point_pre = low_back(matmul(cropped, point_weight) + point_bias)
    point_act = low(jax.nn.gelu(point_pre))
    logits = low_back(matmul(point_act, head_weight[species_id]))
    limit = jnp.where(species_id == 0, TRK, TRK_M)
    track_mask = (jnp.arange(TRK) < limit).astype(jnp.float32)
    return jax.nn.softplus(logits) * track_mask

def forward(inputs, params, crop_start, rel_bucket):
    channel_average = lax.optimization_barrier(jnp.mean(inputs, axis=(0, 1, 2)))
    inverse_deviation = lax.rsqrt(lax.optimization_barrier(jnp.mean(inputs * inputs, axis=(0, 1, 2))) - channel_average * channel_average + EPSILON)
    flat = inputs.reshape(2 * GSEQ, LEN, C)
    species = (jnp.arange(2 * GSEQ) // GSEQ).astype(jnp.int32)
    offsets = crop_start.reshape(2 * GSEQ).astype(jnp.int32)

    def sequence_step(entries):
        return sequence_forward(params, rel_bucket, entries[0], entries[1], entries[2], channel_average, inverse_deviation)
    preds = lax.map(jax.checkpoint(sequence_step), (flat, species, offsets))
    return preds.reshape(2, GSEQ, CROP, TRK)

def reference(inputs, crop_start, rel_bucket, conv_weight, query_weight, key_weight, value_weight, out_weight, up_weight, down_weight, point_weight, rel_table, bn_gain, bn_shift, conv_bias, attn_gain, attn_shift, ffn_gain, ffn_shift, up_bias, down_bias, point_bias, head_weight, pred_grad):
    params = tuple((weight_arg.astype(jnp.float32) for weight_arg in (conv_weight, query_weight, key_weight, value_weight, out_weight, up_weight, down_weight, point_weight, rel_table, bn_gain, bn_shift, conv_bias, attn_gain, attn_shift, ffn_gain, ffn_shift, up_bias, down_bias, point_bias, head_weight)))

    def wrapped(value_entries, *weights):
        return forward(value_entries, weights, crop_start, rel_bucket)
    preds, back = jax.vjp(wrapped, inputs.astype(jnp.float32), *params)
    grads = back(pred_grad.astype(jnp.float32))
    return (preds.astype(jnp.bfloat16), grads[0], grads[1], grads[2], grads[3], grads[4], grads[5], grads[6], grads[7], grads[8], grads[9], grads[10], grads[11], grads[12], grads[13], grads[14], grads[15], grads[16], grads[17], grads[18], grads[19], grads[20])
```

```python
import jax
import jax.numpy as jnp
from jax import lax
from jax.experimental import pallas as pl
from jax.experimental.pallas import tpu as pltpu
from jax.sharding import PartitionSpec as P

HEADS = 8
QK = 64
V = 192
TRK_M = 1643
WIDTH = 5
NB = 32
EPSILON = 1e-05
ROWS = 128
BLOCK = 512
CONV_CHUNKS = 3
EVERYWHERE = ("species", "dp", "seq")


def _head_lanes(e):
    lane = lax.broadcasted_iota(jnp.int32, (1, 2 * QK), 1)
    return (lane >= QK) == (e == 1)

def _toeplitz(u):
    wide = jnp.broadcast_to(u, (ROWS, u.shape[-1]))
    return pltpu.roll(wide, 0, 1, stride=1, stride_axis=0)

def _soft(q, k, bias):
    s = lax.dot_general(q, k, (((1,), (1,)), ((), ())), preferred_element_type=jnp.float32) + bias
    e = jnp.exp(s - jnp.max(s, axis=-1, keepdims=True))
    return e * (1.0 / jnp.sum(e, axis=-1, keepdims=True))

def _join(first, second):
    lane = lax.broadcasted_iota(jnp.int32, (1, 128), 1)
    return jnp.concatenate([first[:, :128], jnp.where(lane < 64, first[:, 128:], second[:, :128]), second[:, 128:]], axis=1)

def attn_fwd_kernel(q_ref, k_ref, v_ref, u_ref, o_ref):
    rows = q_ref.shape[0]
    length = k_ref.shape[0]
    k = k_ref[...]
    tables = [_toeplitz(u_ref[0, e : e + 1, :]) for e in range(2)]
    for a in range(rows // ROWS):
        at = rows - ROWS * a
        span = slice(ROWS * a, ROWS * (a + 1))
        q = q_ref[span, :]
        outs = []
        for e in range(2):
            qe = jnp.where(_head_lanes(e), q, jnp.zeros_like(q))
            p = _soft(qe, k, tables[e][:, at : at + length]).astype(jnp.bfloat16)
            outs.append(jnp.dot(p, v_ref[:, 128 * e : 128 * e + 256], preferred_element_type=jnp.float32))
        o_ref[span, :] = _join(*outs).astype(o_ref.dtype)

def attn_fwd(q, k, v, u):
    rows, length = q.shape[0], k.shape[0]
    pairs = q.shape[1] // (2 * QK)
    return pl.pallas_call(
        attn_fwd_kernel,
        grid=(pairs,),
        in_specs=[
            pl.BlockSpec((rows, 2 * QK), lambda h: (0, h)),
            pl.BlockSpec((length, 2 * QK), lambda h: (0, h)),
            pl.BlockSpec((length, 2 * V), lambda h: (0, h)),
            pl.BlockSpec((1, 2, u.shape[-1]), lambda h: (h, 0, 0)),
        ],
        out_specs=pl.BlockSpec((rows, 2 * V), lambda h: (0, h)),
        out_shape=jax.ShapeDtypeStruct((rows, v.shape[1]), jnp.bfloat16),
        compiler_params=pltpu.CompilerParams(vmem_limit_bytes=48 * 2**20),
        name="attention_forward",
    )(q, k, v, u)

def attn_bwd_kernel(q_ref, k_ref, v_ref, u_ref, g_ref, dq_ref, dk_ref, dv_ref, du_ref, p_scr, s_scr, d_scr):
    rows = q_ref.shape[0]
    length = k_ref.shape[0]
    k = k_ref[...]
    lane2 = lax.broadcasted_iota(jnp.int32, (1, 256), 1)
    dqs, dks, dvs = [], [], []
    for e in range(2):
        table = _toeplitz(u_ref[0, e : e + 1, :])
        d_scr[...] = jnp.zeros_like(d_scr)
        keep = (lane2 < 192) if e == 0 else (lane2 >= 64)
        vcols = slice(128 * e, 128 * e + 256)
        for a in range(rows // ROWS):
            at = rows - ROWS * a
            span = slice(ROWS * a, ROWS * (a + 1))
            q = q_ref[span, :]
            qe = jnp.where(_head_lanes(e), q, jnp.zeros_like(q))
            p = _soft(qe, k, table[:, at : at + length])
            g = g_ref[span, vcols]
            g = jnp.where(keep, g, jnp.zeros_like(g))
            dp = lax.dot_general(g, v_ref[:, vcols], (((1,), (1,)), ((), ())), preferred_element_type=jnp.float32)
            ds = p * (dp - jnp.sum(p * dp, axis=-1, keepdims=True))
            p_scr[span, :] = p.astype(jnp.bfloat16)
            s_scr[span, :] = ds.astype(jnp.bfloat16)
            d_scr[:, at : at + length] += ds
        ds = s_scr[...]
        dqs.append(jnp.dot(ds, k, preferred_element_type=jnp.float32))
        dks.append(lax.dot_general(ds, q_ref[...], (((0,), (0,)), ((), ())), preferred_element_type=jnp.float32))
        dvs.append(lax.dot_general(p_scr[...], g_ref[:, vcols], (((0,), (0,)), ((), ())), preferred_element_type=jnp.float32))
        fold = d_scr[...]
        width = fold.shape[1]
        step = ROWS // 2
        while step:
            fold = fold[:step] + pltpu.roll(fold[step:], width - step, 1)
            step //= 2
        du_ref[0, e : e + 1, :] = fold
    lane = lax.broadcasted_iota(jnp.int32, (1, 128), 1)
    dq_ref[...] = (jnp.where(lane < QK, dqs[0], dqs[1]) * QK ** (-0.5)).astype(dq_ref.dtype)
    dk_ref[...] = jnp.where(lane < QK, dks[0], dks[1]).astype(dk_ref.dtype)
    dv_ref[...] = _join(*dvs).astype(dv_ref.dtype)

def attn_bwd(q, k, v, u, g):
    rows, length = q.shape[0], k.shape[0]
    pairs = q.shape[1] // (2 * QK)
    specs = [
            pl.BlockSpec((rows, 2 * QK), lambda h: (0, h)),
            pl.BlockSpec((length, 2 * QK), lambda h: (0, h)),
            pl.BlockSpec((length, 2 * V), lambda h: (0, h)),
            pl.BlockSpec((1, 2, u.shape[-1]), lambda h: (h, 0, 0)),
            ]
    return pl.pallas_call(
        attn_bwd_kernel,
        grid=(pairs,),
        in_specs=specs + [pl.BlockSpec((rows, 2 * V), lambda h: (0, h))],
        out_specs=specs,
        out_shape=[jax.ShapeDtypeStruct(q.shape, jnp.bfloat16), jax.ShapeDtypeStruct(k.shape, jnp.bfloat16), jax.ShapeDtypeStruct(v.shape, jnp.bfloat16), jax.ShapeDtypeStruct(u.shape, jnp.float32)],
        scratch_shapes=[pltpu.VMEM((rows, length), jnp.bfloat16), pltpu.VMEM((rows, length), jnp.bfloat16), pltpu.VMEM((ROWS, u.shape[-1]), jnp.float32)],
        compiler_params=pltpu.CompilerParams(vmem_limit_bytes=56 * 2**20),
        name="attention_backward",
    )(q, k, v, u, g)


def flip(x, bit):
    peers = lax.axis_size("seq")
    return lax.ppermute(x, "seq", [(i, i ^ bit) for i in range(peers)])


def swap_cores(x):
    return lax.ppermute(x, "species", [(0, 1), (1, 0)])


def to_upper_core(x):
    return lax.ppermute(x, "species", [(0, 1)])


def to_lower_core(x):
    return lax.ppermute(x, "species", [(1, 0)])


def pick(x, index, axis=0):
    return lax.dynamic_index_in_dim(x, index, axis, keepdims=False)


def sort_copies(moves, out_shapes, *pieces):
    def kernel(*refs):
        ins, refs = refs[: len(pieces)], refs[len(pieces) :]
        outs, refs = refs[: len(out_shapes)], refs[len(out_shapes) :]
        stages, (in_sems, out_sems) = refs[: len(out_shapes)], refs[len(out_shapes) :]
        place = {axis: lax.axis_index(axis) for axis in EVERYWHERE}
        arrivals, departures = [], []
        for i, (piece, source, array, target) in enumerate(moves(place)):
            stage = stages[array].at[target]
            arrivals.append(pltpu.make_async_copy(ins[piece].at[source], stage, in_sems.at[i]))
            departures.append(
                pltpu.make_async_copy(stage, outs[array].at[target], out_sems.at[i])
            )
        for copy in arrivals:
            copy.start()
        for arrival, departure in zip(arrivals, departures):
            arrival.wait()
            departure.start()
        for copy in departures:
            copy.wait()

    count = len(moves({axis: 0 for axis in EVERYWHERE}))
    held = sum(x.size * 4 for x in out_shapes) // 2
    return pl.pallas_call(
        kernel,
        in_specs=[pl.BlockSpec(memory_space=pl.ANY)] * len(pieces),
        out_specs=[pl.BlockSpec(memory_space=pl.ANY)] * len(out_shapes),
        out_shape=out_shapes,
        scratch_shapes=[pltpu.VMEM(x.shape, x.dtype) for x in out_shapes]
        + [pltpu.SemaphoreType.DMA((count,))] * 2,
        compiler_params=pltpu.CompilerParams(vmem_limit_bytes=held * 2 + 4 * 2**20),
        cost_estimate=pl.CostEstimate(flops=0, bytes_accessed=held * 2, transcendentals=0),
        name="sort_copies",
    )(*pieces)


def gather_all(shard, first, second, direct, widths=None):
    peers = lax.axis_size("dp")
    rows, columns = shard.shape
    widths = widths or [columns]
    if direct:
        pieces = [shard] + [
            lax.ppermute(shard, "dp", [(i, (i + k) % peers) for i in range(peers)])
            for k in range(1, peers)
        ]
        column = jnp.stack(pieces)
    else:
        column = lax.all_gather(shard, "dp")
    near = jnp.stack([column, flip(column, first)])
    far = flip(near, second)
    near_other = swap_cores(near)
    far_other = swap_cores(far)

    def moves(place):
        mine, seq, z = place["species"], place["seq"], place["dp"]
        found = []
        for piece, core, turn in (
            (0, mine, 0), (1, mine, second), (2, 1 - mine, 0), (3, 1 - mine, second)
        ):
            for m, bit in ((0, 0), (1, first)):
                home = seq ^ (turn ^ bit)
                begin = 0
                for array, width in enumerate(widths):
                    span = pl.ds(begin, width)
                    begin += width
                    if direct:
                        for k in range(peers):
                            at = lax.rem(z + (peers - k), peers)
                            found.append((piece, (m, k, slice(None), span), array, (core, at, home)))
                    else:
                        everything = slice(None)
                        found.append(
                            (piece, (m, everything, everything, span), array, (core, everything, home))
                        )
        return found

    outs = sort_copies(
        moves,
        [jax.ShapeDtypeStruct((2, peers, 4, rows, width), shard.dtype) for width in widths],
        near,
        far,
        near_other,
        far_other,
    )
    return [out.reshape(2 * peers * 4 * rows, out.shape[-1]) for out in outs]


def scatter_all(grad, first, second, direct):
    mine, place, z = lax.axis_index("species"), lax.axis_index("seq"), lax.axis_index("dp")
    peers = lax.axis_size("dp")
    low = jnp.bfloat16
    wide = jnp.float32
    half = (pick(grad, mine).astype(wide) + swap_cores(pick(grad, 1 - mine)).astype(wide)).astype(low)
    for bit in (first, second):
        axis = 1 if bit == 2 or half.ndim == 4 else 2
        here = lax.rem(lax.div(place, bit), 2)
        away = flip(pick(half, 1 - here, axis), bit)
        half = (pick(half, here, axis).astype(wide) + away.astype(wide)).astype(low)
    if direct:
        total = pick(half, z).astype(wide)
        for k in range(1, peers):
            sent = pick(half, lax.rem(z + k, peers))
            total = total + lax.ppermute(
                sent, "dp", [(i, (i + k) % peers) for i in range(peers)]
            ).astype(wide)
        return total
    return lax.psum_scatter(half, "dp", scatter_dimension=0, tiled=False).astype(wide)


def gather_plane(x):
    rows = x.shape[0]
    half = rows // 2
    from_x = flip(x, 1)
    from_y = flip(x, 2)
    top = flip(from_x[:half], 2)
    bottom = flip(from_y[half:], 1)

    def moves(place):
        seq = place["seq"]
        everything = slice(None)
        return [
            (0, (everything,), 0, (seq,)),
            (1, (everything,), 0, (seq ^ 1,)),
            (2, (everything,), 0, (seq ^ 2,)),
            (3, (everything,), 0, (seq ^ 3, pl.ds(0, half))),
            (4, (everything,), 0, (seq ^ 3, pl.ds(half, half))),
        ]

    out = sort_copies(
        moves, [jax.ShapeDtypeStruct((4,) + x.shape, x.dtype)], x, from_x, from_y, top, bottom
    )[0]
    return out.reshape((4 * rows,) + x.shape[1:])


def scatter_plane(x):
    place = lax.axis_index("seq")
    rows, columns = x.shape[0] // 4, x.shape[1]
    half = rows // 2
    low = jnp.bfloat16
    wide = jnp.float32
    parts = x.reshape(4, 2, half, columns)

    def block(toward, which):
        return lax.dynamic_slice(
            parts, (lax.bitwise_xor(place, toward), which, 0, 0), (1, 1, half, columns)
        )[0, 0]

    sums = []
    for which, first, second in ((0, 1, 2), (1, 2, 1)):
        away = flip(jnp.stack([block(first, which), block(3, which)]), first).astype(wide)
        mine = block(0, which).astype(wide) + away[0]
        onward = (block(second, which).astype(wide) + away[1]).astype(low)
        sums.append(mine + flip(onward, second).astype(wide))
    return jnp.concatenate(sums, axis=0)


def exchange_plane(x):
    place = lax.axis_index("seq")
    arrived = [pick(x, place)] + [
        flip(pick(x, lax.bitwise_xor(place, bit)), bit) for bit in (1, 2, 3)
    ]
    stacked = jnp.stack(arrived)
    return jnp.stack([pick(stacked, lax.bitwise_xor(place, j)) for j in range(4)])


def sum_everywhere(x):
    x = x + swap_cores(x)
    x = x + flip(x, 1)
    x = x + flip(x, 2)
    peers = lax.axis_size("dp")
    step = 1
    while step < peers:
        x = x + lax.ppermute(x, "dp", [(i, i ^ step) for i in range(peers)])
        step *= 2
    return x


def with_halo(cells, width):
    count = lax.axis_size("seq")
    head, tail = cells[:width], cells[-width:]
    up = lax.ppermute(tail, "seq", [(i, i + 1) for i in range(count - 1)])
    down = lax.ppermute(head, "seq", [(i + 1, i) for i in range(count - 1)])
    return jnp.concatenate([up, cells, down], axis=0)


def spread_tracks(x):
    rows = x.shape[0]
    lower = lax.axis_index("species") == 0
    human = jnp.pad(x, ((0, 0), (0, 12 * BLOCK - x.shape[1]))).reshape(rows, 4, 3, BLOCK)
    human = human.transpose(1, 2, 0, 3)
    mouse = x[:, : 4 * BLOCK].reshape(rows, 4, BLOCK).transpose(1, 0, 2)
    other = to_upper_core(human[:, 2])
    first = jnp.where(lower, human[:, 0], other)
    second = jnp.where(lower, human[:, 1], mouse)
    return jnp.concatenate([first, second], axis=-1)


def collect_tracks(x, tracks):
    rows = x.shape[1]
    lower = lax.axis_index("species") == 0
    other = to_lower_core(x[:, :, :BLOCK])
    human = jnp.stack([x[:, :, :BLOCK], x[:, :, BLOCK:], other], axis=1)
    human = human.transpose(2, 0, 1, 3).reshape(rows, 12 * BLOCK)[:, :tracks]
    mouse = x[:, :, BLOCK:].transpose(1, 0, 2).reshape(rows, 4 * BLOCK)
    mouse = jnp.pad(mouse, ((0, 0), (0, tracks - 4 * BLOCK)))
    return jnp.where(lower, human, mouse)


def layer_norm(value_entries, gain, shift):
    centre = jnp.mean(value_entries, axis=-1, keepdims=True)
    centred = value_entries - centre
    spread = jnp.mean(centred * centred, axis=-1, keepdims=True)
    return centred * lax.rsqrt(spread + EPSILON) * gain + shift


def gelu_back(pre, upstream):
    _, back = jax.vjp(jax.nn.gelu, pre)
    return back(upstream)[0]


def dense(left, right):
    return jnp.dot(left, right, preferred_element_type=jnp.float32)


def dense_back(left, right):
    return lax.dot_general(
        left, right, (((1,), (1,)), ((), ())), preferred_element_type=jnp.float32
    )


def outer_sum(left, right):
    return lax.dot_general(
        left, right, (((0,), (0,)), ((), ())), preferred_element_type=jnp.float32
    )


def row_sum(value_entries):
    return jnp.sum(value_entries.astype(jnp.float32), axis=0)


def on_device(
    inputs,
    crop_start,
    rel_bucket,
    conv_weight,
    query_weight,
    key_weight,
    value_weight,
    out_weight,
    up_weight,
    down_weight,
    point_weight,
    rel_table,
    bn_gain,
    bn_shift,
    conv_bias,
    attn_gain,
    attn_shift,
    ffn_gain,
    ffn_shift,
    up_bias,
    down_bias,
    point_bias,
    head_weight,
    pred_grad,
):
    low = jnp.bfloat16
    wide = jnp.float32
    bin_count, chans = inputs.shape[2], inputs.shape[3]
    tracks = head_weight.shape[2]
    crop_rows = 4 * pred_grad.shape[2]
    seq_pos = lax.axis_index("seq")
    species_id = lax.axis_index("species")
    lower = species_id == 0
    dp_count = lax.axis_size("dp")
    device_count = 2 * dp_count * 4
    portion_index = lax.axis_index(EVERYWHERE)
    full_len = 4 * bin_count
    element_count = float(device_count * bin_count)
    half_width = WIDTH // 2

    value_entries = inputs[0, 0].astype(wide)
    small = (
        bn_gain, bn_shift, conv_bias, attn_gain, attn_shift, ffn_gain, ffn_shift, up_bias, down_bias,
        point_bias, rel_table,
    )

    def placed(x):
        whole = jnp.zeros((device_count * x.shape[0],), wide)
        return lax.dynamic_update_slice_in_dim(whole, x.astype(wide), portion_index * x.shape[0], 0)

    joined = jnp.concatenate(
        [jnp.sum(value_entries, axis=0), jnp.sum(value_entries * value_entries, axis=0)]
        + [placed(x) for x in small]
    )
    joined = sum_everywhere(joined.reshape(-1, 128)).reshape(-1)
    moment_one, moment_two = joined[:chans], joined[chans : 2 * chans]
    at = 2 * chans
    whole_small = []
    for x in small:
        size = device_count * x.shape[0]
        whole_small.append(joined[at : at + size])
        at += size
    (
        batchnorm_gain, batchnorm_shift, bias_conv, gain_attn, shift_attn, gain_ffn, shift_ffn, bias_up,
        bias_down, bias_point, table_flat,
    ) = whole_small

    chunk = chans // CONV_CHUNKS
    conv_parts = [
        gather_all(conv_weight[:, i * chunk : (i + 1) * chunk], *((2, 1) if i % 2 else (1, 2)), True)[0]
        for i in range(CONV_CHUNKS)
    ]
    w_query, w_key, w_value, w_out = gather_all(
        jnp.concatenate([query_weight, key_weight, value_weight, out_weight], axis=1),
        2,
        1,
        False,
        [x.shape[1] for x in (query_weight, key_weight, value_weight, out_weight)],
    )
    (w_up,) = gather_all(up_weight, 1, 2, False)
    (w_down,) = gather_all(down_weight, 2, 1, False)
    (w_point,) = gather_all(point_weight, 1, 2, False)
    spread = exchange_plane(
        spread_tracks(jnp.concatenate([head_weight[0], pred_grad[0, 0]], axis=0))
    )
    head_rows = head_weight.shape[1]
    w_head = lax.all_gather(spread[:, :head_rows], "dp").reshape(-1, 2 * BLOCK)
    track_grad = spread[:, head_rows:].reshape(crop_rows, 2 * BLOCK)

    channel_average = moment_one / element_count
    inverse_deviation = lax.rsqrt(
        moment_two / element_count - channel_average * channel_average + EPSILON
    )
    standardized_input = (value_entries - channel_average) * inverse_deviation
    normed_rows = standardized_input * batchnorm_gain + batchnorm_shift
    activity = jax.nn.gelu(normed_rows).astype(low)
    act_pad = with_halo(activity, half_width)
    act_taps = jnp.concatenate([act_pad[k : k + bin_count] for k in range(WIDTH)], axis=1)
    conv_out = bias_conv + jnp.concatenate([dense(act_taps, w) for w in conv_parts], axis=1)
    first_sum = value_entries + conv_out
    normed_one = layer_norm(first_sum, gain_attn, shift_attn).astype(low)
    scale = QK ** (-0.5)
    query_rows = (dense(normed_one, w_query).astype(low).astype(wide) * scale).astype(low)
    key_rows = dense(normed_one, w_key).astype(low)
    value_rows = dense(normed_one, w_value).astype(low)
    key_all = gather_plane(key_rows)
    value_all = gather_plane(value_rows)
    bucket_window = lax.dynamic_slice_in_dim(
        jnp.pad(rel_bucket, (1, 0), constant_values=-1),
        full_len - bin_count - seq_pos * bin_count,
        full_len + bin_count,
    )
    window_onehot = (bucket_window[:, None] == jnp.arange(NB)[None, :]).astype(wide)
    distance_bias = lax.dot_general(
        table_flat.reshape(HEADS, NB), window_onehot, (((1,), (1,)), ((), ())),
        precision=lax.Precision.HIGHEST, preferred_element_type=wide,
    ).reshape(HEADS // 2, 2, full_len + bin_count)
    mixed = attn_fwd(query_rows, key_all, value_all, distance_bias)
    second_sum = first_sum + dense(mixed, w_out)
    normed_two = layer_norm(second_sum, gain_ffn, shift_ffn).astype(low)
    up_pre = dense(normed_two, w_up) + bias_up
    up_act = jax.nn.gelu(up_pre).astype(low)
    third_sum = second_sum + dense(up_act, w_down) + bias_down
    third_all = gather_plane(third_sum.astype(low))
    crop_at = crop_start[0, 0]
    cropped = lax.dynamic_slice_in_dim(third_all, crop_at, crop_rows, 0)
    point_pre = dense(cropped, w_point) + bias_point
    point_act = jax.nn.gelu(point_pre).astype(low)

    human_act = jnp.where(lower, point_act, to_upper_core(point_act))
    column = jnp.arange(BLOCK)
    first_valid = 3 * BLOCK * seq_pos + jnp.where(lower, 0, 2 * BLOCK) + column < tracks
    second_valid = jnp.where(
        lower, 3 * BLOCK * seq_pos + BLOCK + column < tracks, BLOCK * seq_pos + column < TRK_M
    )
    preds, head_grads, logit_grads = [], [], []
    for which, act, valid in ((0, human_act, first_valid), (1, point_act, second_valid)):
        span = slice(which * BLOCK, (which + 1) * BLOCK)
        mask = valid.astype(wide)
        logits = dense(act, w_head[:, span])
        preds.append((jax.nn.softplus(logits) * mask).astype(low))
        logit_grad = (track_grad[:, span].astype(wide) * mask * jax.nn.sigmoid(logits)).astype(low)
        logit_grads.append(logit_grad)
        head_grads.append(outer_sum(act, logit_grad).astype(low))
    first_back = dense_back(logit_grads[0], w_head[:, :BLOCK])
    second_back = dense_back(logit_grads[1], w_head[:, BLOCK:])
    point_act_grad = second_back + jnp.where(
        lower, first_back + to_lower_core(first_back.astype(low)).astype(wide), 0.0
    )
    predictions = collect_tracks(
        exchange_plane(jnp.concatenate(preds, axis=1).reshape(4, crop_rows // 4, 2 * BLOCK)), tracks
    )

    point_grad = gelu_back(point_pre, point_act_grad).astype(low)
    crop_grad = dense_back(point_grad, w_point).astype(low)
    third_part = lax.dynamic_update_slice_in_dim(
        jnp.zeros((full_len, chans), low), crop_grad, crop_at, 0
    )
    third_grad = scatter_plane(third_part)
    grid_shape = (2, dp_count, 2, 2)

    def blocks(grad):
        return grad.astype(low).reshape(grid_shape + (grad.shape[0] // device_count, grad.shape[1]))

    head_sum = lax.psum_scatter(
        jnp.concatenate(head_grads, axis=1).reshape(dp_count, 4 * head_rows, 2 * BLOCK),
        "dp", scatter_dimension=0, tiled=False,
    )
    head_grad = collect_tracks(
        exchange_plane(head_sum.reshape(4, head_rows, 2 * BLOCK)), tracks
    ).astype(wide)
    grad_point_w = scatter_all(blocks(outer_sum(cropped, point_grad)), 1, 2, False)
    grad_point_b = row_sum(point_grad)
    down_grad = third_grad.astype(low)
    grad_down_w = scatter_all(blocks(outer_sum(up_act, down_grad)), 2, 1, False)
    grad_down_b = row_sum(down_grad)
    up_grad = gelu_back(up_pre, dense_back(down_grad, w_down)).astype(low)
    grad_up_w = scatter_all(blocks(outer_sum(normed_two, up_grad)), 1, 2, False)
    grad_up_b = row_sum(up_grad)
    _, norm_two_back = jax.vjp(layer_norm, second_sum, gain_ffn, shift_ffn)
    second_part, grad_ffn_gain, grad_ffn_shift = norm_two_back(dense_back(up_grad, w_up))
    second_grad = third_grad + second_part
    out_grad = second_grad.astype(low)
    grad_out_w = outer_sum(mixed, out_grad)
    mixed_grad = dense_back(out_grad, w_out).astype(low)
    query_low, key_part, value_part, distance_grad = attn_bwd(
        query_rows, key_all, value_all, distance_bias, mixed_grad
    )
    grad_table = jnp.dot(
        distance_grad.reshape(HEADS, -1), window_onehot, precision=lax.Precision.HIGHEST,
        preferred_element_type=wide,
    ).reshape(HEADS * NB)
    key_low = scatter_plane(key_part).astype(low)
    value_low = scatter_plane(value_part).astype(low)
    grad_qkvo = scatter_all(
        blocks(
            jnp.concatenate(
                [outer_sum(normed_one, x) for x in (query_low, key_low, value_low)] + [grad_out_w],
                axis=1,
            )
        ),
        2,
        1,
        False,
    )
    normed_one_grad = (
        dense_back(query_low, w_query) + dense_back(key_low, w_key) + dense_back(value_low, w_value)
    )
    _, norm_one_back = jax.vjp(layer_norm, first_sum, gain_attn, shift_attn)
    first_part, grad_attn_gain, grad_attn_shift = norm_one_back(normed_one_grad)
    first_grad = second_grad + first_part
    conv_grad = first_grad.astype(low)
    grad_conv_b = row_sum(conv_grad)
    grad_conv_w = jnp.concatenate(
        [
            scatter_all(
                blocks(outer_sum(act_taps, conv_grad[:, i * chunk : (i + 1) * chunk])),
                *((2, 1) if i % 2 else (1, 2)),
                True,
            )
            for i in range(CONV_CHUNKS)
        ],
        axis=1,
    )
    grad_pad = with_halo(conv_grad, half_width)
    act_grad = jnp.zeros((bin_count, chans), wide)
    for tap_index in range(WIDTH):
        begin = 2 * half_width - tap_index
        rows = grad_pad[begin : begin + bin_count]
        for i, w in enumerate(conv_parts):
            act_grad = act_grad + dense_back(
                rows[:, i * chunk : (i + 1) * chunk], w[tap_index * chans : (tap_index + 1) * chans]
            )
    normed_rows_gradient = gelu_back(normed_rows, act_grad)
    vectors = (
        jnp.sum(normed_rows_gradient * standardized_input, axis=0),
        jnp.sum(normed_rows_gradient, axis=0),
        grad_table,
        grad_conv_b,
        grad_attn_gain,
        grad_attn_shift,
        grad_ffn_gain,
        grad_ffn_shift,
        grad_up_b,
        grad_down_b,
        grad_point_b,
    )
    summed = sum_everywhere(jnp.concatenate(vectors).reshape(-1, 128)).reshape(-1)
    standardized_sum, plain_gradient_sum = summed[:chans], summed[chans : 2 * chans]
    input_grad = first_grad + batchnorm_gain * inverse_deviation * (
        normed_rows_gradient
        - plain_gradient_sum / element_count
        - standardized_input * standardized_sum / element_count
    )
    shares = []
    at = 0
    for x in vectors:
        size = x.shape[0] // device_count
        shares.append(lax.dynamic_slice_in_dim(summed, at + portion_index * size, size))
        at += x.shape[0]
    bn_gain_share, bn_shift_share, table_share, conv_b_share = shares[:4]
    attn_gain_share, attn_shift_share, ffn_gain_share, ffn_shift_share = shares[4:8]
    up_b_share, down_b_share, point_b_share = shares[8:]
    ends = [0]
    for x in (query_weight, key_weight, value_weight, out_weight):
        ends.append(ends[-1] + x.shape[1])
    query_share, key_share, value_share, out_share = (
        grad_qkvo[:, ends[i] : ends[i + 1]] for i in range(4)
    )
    return (
        predictions[None, None],
        input_grad[None, None],
        grad_conv_w,
        query_share,
        key_share,
        value_share,
        out_share,
        grad_up_w,
        grad_down_w,
        grad_point_w,
        table_share,
        bn_gain_share,
        bn_shift_share,
        conv_b_share,
        attn_gain_share,
        attn_shift_share,
        ffn_gain_share,
        ffn_shift_share,
        up_b_share,
        down_b_share,
        point_b_share,
        head_grad[None],
    )


def solution(mesh):
    everywhere = P(EVERYWHERE)
    rows = P(EVERYWHERE, None)
    bins = P("species", "dp", "seq", None)
    head = P("species", ("dp", "seq"), None)
    return jax.shard_map(
        on_device,
        mesh=mesh,
        in_specs=(bins, P("species", "dp"), P()) + (rows,) * 8 + (everywhere,) * 11 + (head, bins),
        out_specs=(bins, bins) + (rows,) * 8 + (everywhere,) * 11 + (head,),
        check_vma=False,
    )
```

```python
import jax
import jax.numpy as jnp
from jax import lax
from jax.experimental import pallas as pl
from jax.experimental.pallas import tpu as pltpu
from jax.sharding import PartitionSpec as P

HEADS = 8
QK = 64
V = 192
TRK_M = 1643
WIDTH = 5
NB = 32
EPSILON = 1e-05
ROWS = 128
BLOCK = 512
TILE = 256
EVERYWHERE = ("species", "dp", "seq")


def _head_lanes(e):
    lane = lax.broadcasted_iota(jnp.int32, (1, 2 * QK), 1)
    return (lane >= QK) == (e == 1)

def _toeplitz(u):
    wide = jnp.broadcast_to(u, (ROWS, u.shape[-1]))
    return pltpu.roll(wide, 0, 1, stride=1, stride_axis=0)

def _soft(q, k, bias):
    s = lax.dot_general(q, k, (((1,), (1,)), ((), ())), preferred_element_type=jnp.float32) + bias
    e = jnp.exp(s - jnp.max(s, axis=-1, keepdims=True))
    return e * (1.0 / jnp.sum(e, axis=-1, keepdims=True))

def _join(first, second):
    lane = lax.broadcasted_iota(jnp.int32, (1, 128), 1)
    return jnp.concatenate([first[:, :128], jnp.where(lane < 64, first[:, 128:], second[:, :128]), second[:, 128:]], axis=1)

def attn_fwd_kernel(q_ref, kv_ref, u_ref, o_ref):
    rows = q_ref.shape[0]
    length = kv_ref.shape[0]
    k = kv_ref[:, : 2 * QK]
    tables = [_toeplitz(u_ref[0, e : e + 1, :]) for e in range(2)]
    for a in range(rows // ROWS):
        at = rows - ROWS * a
        span = slice(ROWS * a, ROWS * (a + 1))
        q = q_ref[span, :]
        outs = []
        for e in range(2):
            qe = jnp.where(_head_lanes(e), q, jnp.zeros_like(q))
            p = _soft(qe, k, tables[e][:, at : at + length]).astype(jnp.bfloat16)
            outs.append(jnp.dot(p, kv_ref[:, 128 * e + 128 : 128 * e + 384], preferred_element_type=jnp.float32))
        o_ref[span, :] = _join(*outs).astype(o_ref.dtype)

PAIR = 2 * QK + 2 * V


def attn_fwd(q, kv, u):
    rows, length = q.shape[0], kv.shape[0]
    pairs = q.shape[1] // (2 * QK)
    return pl.pallas_call(
        attn_fwd_kernel,
        grid=(pairs,),
        in_specs=[
            pl.BlockSpec((rows, 2 * QK), lambda h: (0, h)),
            pl.BlockSpec((length, PAIR), lambda h: (0, h)),
            pl.BlockSpec((1, 2, u.shape[-1]), lambda h: (h, 0, 0)),
        ],
        out_specs=pl.BlockSpec((rows, 2 * V), lambda h: (0, h)),
        out_shape=jax.ShapeDtypeStruct((rows, pairs * 2 * V), jnp.bfloat16),
        compiler_params=pltpu.CompilerParams(vmem_limit_bytes=48 * 2**20),
        cost_estimate=pl.CostEstimate(
            flops=0, bytes_accessed=0, transcendentals=0
        ),
        name="attention_forward",
    )(q, kv, u)


def attn_bwd_kernel(
    q_ref, kv_ref, u_ref, g_ref, dq_ref, dkv_ref, du_ref, p_scr, s_scr, d_scr
):
    rows = q_ref.shape[0]
    length = kv_ref.shape[0]
    k = kv_ref[:, : 2 * QK]
    lane2 = lax.broadcasted_iota(jnp.int32, (1, 256), 1)
    dqs, dks, dvs = [], [], []
    for e in range(2):
        table = _toeplitz(u_ref[0, e : e + 1, :])
        d_scr[...] = jnp.zeros_like(d_scr)
        keep = (lane2 < 192) if e == 0 else (lane2 >= 64)
        vcols = slice(128 * e, 128 * e + 256)
        for a in range(rows // ROWS):
            at = rows - ROWS * a
            span = slice(ROWS * a, ROWS * (a + 1))
            q = q_ref[span, :]
            qe = jnp.where(_head_lanes(e), q, jnp.zeros_like(q))
            p = _soft(qe, k, table[:, at : at + length])
            g = g_ref[span, vcols]
            g = jnp.where(keep, g, jnp.zeros_like(g))
            dp = lax.dot_general(g, kv_ref[:, 128 * e + 128 : 128 * e + 384], (((1,), (1,)), ((), ())), preferred_element_type=jnp.float32)
            ds = p * (dp - jnp.sum(p * dp, axis=-1, keepdims=True))
            p_scr[span, :] = p.astype(jnp.bfloat16)
            s_scr[span, :] = ds.astype(jnp.bfloat16)
            d_scr[:, at : at + length] += ds
        ds = s_scr[...]
        dqs.append(jnp.dot(ds, k, preferred_element_type=jnp.float32))
        dks.append(lax.dot_general(ds, q_ref[...], (((0,), (0,)), ((), ())), preferred_element_type=jnp.float32))
        dvs.append(lax.dot_general(p_scr[...], g_ref[:, vcols], (((0,), (0,)), ((), ())), preferred_element_type=jnp.float32))
        fold = d_scr[...]
        width = fold.shape[1]
        step = ROWS // 2
        while step:
            fold = fold[:step] + pltpu.roll(fold[step:], width - step, 1)
            step //= 2
        du_ref[0, e : e + 1, :] = fold
    lane = lax.broadcasted_iota(jnp.int32, (1, 128), 1)
    dq_ref[...] = (jnp.where(lane < QK, dqs[0], dqs[1]) * QK ** (-0.5)).astype(dq_ref.dtype)
    dkv_ref[:, : 2 * QK] = jnp.where(lane < QK, dks[0], dks[1]).astype(dkv_ref.dtype)
    dkv_ref[:, 2 * QK :] = _join(*dvs).astype(dkv_ref.dtype)

def attn_bwd(q, kv, u, g):
    rows, length = q.shape[0], kv.shape[0]
    pairs = q.shape[1] // (2 * QK)
    specs = [
        pl.BlockSpec((rows, 2 * QK), lambda h: (0, h)),
        pl.BlockSpec((length, PAIR), lambda h: (0, h)),
        pl.BlockSpec((1, 2, u.shape[-1]), lambda h: (h, 0, 0)),
    ]
    return pl.pallas_call(
        attn_bwd_kernel,
        grid=(pairs,),
        in_specs=specs + [pl.BlockSpec((rows, 2 * V), lambda h: (0, h))],
        out_specs=specs,
        out_shape=[
            jax.ShapeDtypeStruct(q.shape, jnp.bfloat16),
            jax.ShapeDtypeStruct(kv.shape, jnp.bfloat16),
            jax.ShapeDtypeStruct(u.shape, jnp.float32),
        ],
        scratch_shapes=[
            pltpu.VMEM((rows, length), jnp.bfloat16),
            pltpu.VMEM((rows, length), jnp.bfloat16),
            pltpu.VMEM((ROWS, u.shape[-1]), jnp.float32),
        ],
        compiler_params=pltpu.CompilerParams(vmem_limit_bytes=56 * 2**20),
        cost_estimate=pl.CostEstimate(
            flops=0, bytes_accessed=0, transcendentals=0
        ),
        name="attention_backward",
    )(q, kv, u, g)


def flip(x, bit):
    peers = lax.axis_size("seq")
    return lax.ppermute(x, "seq", [(i, i ^ bit) for i in range(peers)])


def swap_cores(x):
    return lax.ppermute(x, "species", [(0, 1), (1, 0)])


def to_upper_core(x):
    return lax.ppermute(x, "species", [(0, 1)])


def to_lower_core(x):
    return lax.ppermute(x, "species", [(1, 0)])


def pick(x, index, axis=0):
    return lax.dynamic_index_in_dim(x, index, axis, keepdims=False)


def sort_copies(moves, out_shapes, *pieces):
    def kernel(*refs):
        ins, refs = refs[: len(pieces)], refs[len(pieces) :]
        outs, refs = refs[: len(out_shapes)], refs[len(out_shapes) :]
        stages, (in_sems, out_sems) = refs[: len(out_shapes)], refs[len(out_shapes) :]
        place = {axis: lax.axis_index(axis) for axis in EVERYWHERE}
        arrivals, departures = [], []
        for i, (piece, source, array, target) in enumerate(moves(place)):
            stage = stages[array].at[target]
            arrivals.append(pltpu.make_async_copy(ins[piece].at[source], stage, in_sems.at[i]))
            departures.append(
                pltpu.make_async_copy(stage, outs[array].at[target], out_sems.at[i])
            )
        for copy in arrivals:
            copy.start()
        for arrival, departure in zip(arrivals, departures):
            arrival.wait()
            departure.start()
        for copy in departures:
            copy.wait()

    count = len(moves({axis: 0 for axis in EVERYWHERE}))
    held = sum(x.size * 4 for x in out_shapes) // 2
    return pl.pallas_call(
        kernel,
        in_specs=[pl.BlockSpec(memory_space=pl.ANY)] * len(pieces),
        out_specs=[pl.BlockSpec(memory_space=pl.ANY)] * len(out_shapes),
        out_shape=out_shapes,
        scratch_shapes=[pltpu.VMEM(x.shape, x.dtype) for x in out_shapes]
        + [pltpu.SemaphoreType.DMA((count,))] * 2,
        compiler_params=pltpu.CompilerParams(vmem_limit_bytes=held * 2 + 4 * 2**20),
        cost_estimate=pl.CostEstimate(flops=0, bytes_accessed=0, transcendentals=0),
        name="sort_copies",
    )(*pieces)


def tie_kernel(*refs):
    del refs


def tie(x, *others):
    if not others:
        return x
    return pl.pallas_call(
        tie_kernel,
        in_specs=[pl.BlockSpec(memory_space=pl.ANY)] * (1 + len(others)),
        out_specs=pl.BlockSpec(memory_space=pl.ANY),
        out_shape=jax.ShapeDtypeStruct(x.shape, x.dtype),
        input_output_aliases={0: 0},
        cost_estimate=pl.CostEstimate(flops=0, bytes_accessed=0, transcendentals=0),
        name="tie",
    )(x, *others)


def beside(column, bit):
    return jnp.stack([column, flip(column, bit)])


def sorted_rows(parts, arrays):
    pieces = []
    for near, far, _, _ in parts:
        pieces += [near, far, swap_cores(near), swap_cores(far)]
    peers, depth = parts[0][0].shape[1:3]

    def moves(place):
        mine, seq = place["species"], place["seq"]
        everything = slice(None)
        found = []
        left = 0
        for part, (near, _, first, second) in enumerate(parts):
            right = left + near.shape[-1]
            runs = []
            for array, (_, _, blocks) in enumerate(arrays):
                for begin, size, which, column in blocks:
                    low, high = max(begin, left), min(begin + size, right)
                    if low < high:
                        source = pl.ds(low - left, high - low)
                        target = pl.ds(column + low - begin, high - low)
                        runs.append((array, source, which, target))
            left = right
            for piece, core, turn in (
                (0, mine, 0), (1, mine, second), (2, 1 - mine, 0), (3, 1 - mine, second)
            ):
                for m, bit in ((0, 0), (1, first)):
                    home = seq ^ (turn ^ bit)
                    for array, source, which, target in runs:
                        found.append(
                            (
                                4 * part + piece,
                                (m, everything, everything, source),
                                array,
                                (core, everything, home, which, everything, target),
                            )
                        )
        return found

    outs = sort_copies(
        moves,
        [
            jax.ShapeDtypeStruct((2, peers, 4, count, depth, width), pieces[0].dtype)
            for count, width, _ in arrays
        ],
        *pieces,
    )
    return [out.reshape(-1, out.shape[-1]) for out in outs]


def place_rows_kernel(at_ref, x_ref, o_ref, padded):
    rows, length, columns = x_ref.shape[0], o_ref.shape[0], o_ref.shape[1]
    margin = length - rows
    padded[...] = jnp.zeros_like(padded)
    padded[margin : margin + rows, :] = x_ref[...].astype(jnp.float32)
    begin = margin - at_ref[0]
    step = lax.rem(begin, 8)
    window = padded[pl.ds(pl.multiple_of(begin - step, 8), length + 8), :]
    turned = pltpu.roll(window.reshape(length // 8 + 1, 8, columns), lax.rem(8 - step, 8), 1)
    row = lax.broadcasted_iota(jnp.int32, (1, 8, columns), 1)
    placed = jnp.where(row < 8 - step, turned[:-1], turned[1:])
    o_ref[...] = placed.reshape(length, columns).astype(o_ref.dtype)


def place_rows(x, at, length):
    rows, columns = x.shape
    wide = 256
    return pl.pallas_call(
        place_rows_kernel,
        grid=(columns // wide,),
        in_specs=[
            pl.BlockSpec(memory_space=pltpu.SMEM),
            pl.BlockSpec((rows, wide), lambda i: (0, i)),
        ],
        out_specs=pl.BlockSpec((length, wide), lambda i: (0, i)),
        out_shape=jax.ShapeDtypeStruct((length, columns), x.dtype),
        scratch_shapes=[pltpu.VMEM((2 * length - rows + 8, wide), jnp.float32)],
        compiler_params=pltpu.CompilerParams(vmem_limit_bytes=32 * 2**20),
        name="place_rows",
    )(at.reshape(1), x)


def both_halves(mine):
    other = swap_cores(mine)

    def moves(place):
        core = place["species"]
        return [(0, (slice(None),), 0, (core,)), (1, (slice(None),), 0, (1 - core,))]

    return sort_copies(moves, [jax.ShapeDtypeStruct((2,) + mine.shape, mine.dtype)], mine, other)[0]


def tracks_grad_kernel(first_ref, second_ref, g_ref, o_ref):
    for which, left in enumerate((first_ref, second_ref)):
        span = slice(which * BLOCK, (which + 1) * BLOCK)
        o_ref[:, span] = lax.dot_general(
            left[...], g_ref[:, span], (((0,), (0,)), ((), ())), preferred_element_type=jnp.float32
        ).astype(o_ref.dtype)


def tracks_grad(first, second, g):
    rows, hidden = first.shape
    return pl.pallas_call(
        tracks_grad_kernel,
        grid=(hidden // TILE,),
        in_specs=[
            pl.BlockSpec((rows, TILE), lambda i: (0, i)),
            pl.BlockSpec((rows, TILE), lambda i: (0, i)),
            pl.BlockSpec((rows, 2 * BLOCK), lambda i: (0, 0)),
        ],
        out_specs=pl.BlockSpec((TILE, 2 * BLOCK), lambda i: (i, 0)),
        out_shape=jax.ShapeDtypeStruct((hidden, 2 * BLOCK), jnp.bfloat16),
        compiler_params=pltpu.CompilerParams(vmem_limit_bytes=32 * 2**20),
        cost_estimate=pl.CostEstimate(flops=0, bytes_accessed=0, transcendentals=0),
        name="tracks_grad",
    )(first, second, g)


def conv_forward_kernel(x_ref, w_ref, o_ref, total):
    length = x_ref.shape[0]
    margin = 8
    total[...] = jnp.zeros_like(total)
    for tap in range(WIDTH):
        for begin in range(0, length, TILE):
            product = jnp.dot(
                x_ref[begin : begin + TILE, :], w_ref[tap], preferred_element_type=jnp.float32
            )
            at = margin + begin + WIDTH // 2 - tap
            total[at : at + TILE, :] += product
    o_ref[...] = total[margin : margin + length, :].astype(o_ref.dtype)


def conv_forward(x, w):
    length, outputs = x.shape[0], w.shape[2]
    return pl.pallas_call(
        conv_forward_kernel,
        out_shape=jax.ShapeDtypeStruct((length, outputs), jnp.bfloat16),
        in_specs=[pl.BlockSpec(memory_space=pltpu.VMEM)] * 2,
        out_specs=pl.BlockSpec(memory_space=pltpu.VMEM),
        scratch_shapes=[pltpu.VMEM((length + 16, outputs), jnp.float32)],
        compiler_params=pltpu.CompilerParams(vmem_limit_bytes=40 * 2**20),
        cost_estimate=pl.CostEstimate(flops=0, bytes_accessed=0, transcendentals=0),
        name="conv_forward",
    )(x, w)


def conv_back_kernel(g_ref, w_ref, o_ref):
    outputs = w_ref.shape[2]
    total = None
    for tap in range(WIDTH):
        term = lax.dot_general(
            g_ref[:, tap * outputs : (tap + 1) * outputs],
            w_ref[tap],
            (((1,), (1,)), ((), ())),
            preferred_element_type=jnp.float32,
        )
        total = term if total is None else total + term
    o_ref[...] = total.astype(o_ref.dtype)


def conv_back(g, w):
    length, chans = g.shape[0], w.shape[1]
    return pl.pallas_call(
        conv_back_kernel,
        grid=(length // TILE,),
        in_specs=[
            pl.BlockSpec((TILE, g.shape[1]), lambda i: (i, 0)),
            pl.BlockSpec(w.shape, lambda i: (0, 0, 0)),
        ],
        out_specs=pl.BlockSpec((TILE, chans), lambda i: (i, 0)),
        out_shape=jax.ShapeDtypeStruct((length, chans), jnp.bfloat16),
        compiler_params=pltpu.CompilerParams(vmem_limit_bytes=40 * 2**20),
        cost_estimate=pl.CostEstimate(flops=0, bytes_accessed=0, transcendentals=0),
        name="conv_back",
    )(g, w)


def outer_kernel(base_ref, left_ref, right_ref, *refs):
    total = lax.dot_general(
        left_ref[...], right_ref[...], (((0,), (0,)), ((), ())), preferred_element_type=jnp.float32
    )
    if len(refs) == 2:
        total = total + refs[0][...].astype(jnp.float32)
    refs[-1][...] = total.astype(refs[-1].dtype)


def outer_half(left, right, which, more=None, taps=1):
    rows, chans = left.shape
    columns = right.shape[1] // taps
    tiles = chans // TILE
    count = taps * tiles // 2
    base = ((lax.axis_index("species") ^ which) * count).reshape(1).astype(jnp.int32)
    out_spec = pl.BlockSpec((TILE, columns), lambda i, at: (i, 0))
    return pl.pallas_call(
        outer_kernel,
        grid_spec=pltpu.PrefetchScalarGridSpec(
            num_scalar_prefetch=1,
            grid=(count,),
            in_specs=[
                pl.BlockSpec((rows, TILE), lambda i, at: (0, lax.rem(at[0] + i, tiles))),
                pl.BlockSpec((rows, columns), lambda i, at: (0, lax.div(at[0] + i, tiles))),
            ]
            + ([] if more is None else [out_spec]),
            out_specs=out_spec,
        ),
        out_shape=jax.ShapeDtypeStruct((count * TILE, columns), jnp.bfloat16),
        compiler_params=pltpu.CompilerParams(vmem_limit_bytes=40 * 2**20),
        cost_estimate=pl.CostEstimate(flops=0, bytes_accessed=0, transcendentals=0),
        name="outer_half",
    )(base, left, right, *([] if more is None else [more]))


def by_device(total):
    peers = lax.axis_size("dp")
    return total.reshape(peers, 2, 2, total.shape[0] // (4 * peers), total.shape[1])


def fold(half, bit):
    axis = 2 if bit == 1 and half.ndim == 5 else 1
    here = lax.rem(lax.div(lax.axis_index("seq"), bit), 2)
    away = flip(pick(half, 1 - here, axis), bit)
    return (pick(half, here, axis).astype(jnp.float32) + away.astype(jnp.float32)).astype(half.dtype)


def fold_both(grads, steps):
    if steps == 0:
        middle = grads.shape[-1] // 2
        return fold(grads[..., :middle], 1), fold(grads[..., middle:], 2)
    return fold(grads[0], 2), fold(grads[1], 1)


def gather_begin(x):
    half = x.shape[0] // 2
    from_x, from_y = flip(x, 1), flip(x, 2)
    return x, from_x, from_y, from_x[:half], from_y[half:]


def gather_end(x, from_x, from_y, top, bottom):
    rows = x.shape[0]
    half = rows // 2
    top, bottom = flip(top, 2), flip(bottom, 1)

    def moves(place):
        seq = place["seq"]
        everything = slice(None)
        return [
            (0, (everything,), 0, (seq,)),
            (1, (everything,), 0, (seq ^ 1,)),
            (2, (everything,), 0, (seq ^ 2,)),
            (3, (everything,), 0, (seq ^ 3, pl.ds(0, half))),
            (4, (everything,), 0, (seq ^ 3, pl.ds(half, half))),
        ]

    out = sort_copies(
        moves, [jax.ShapeDtypeStruct((4,) + x.shape, x.dtype)], x, from_x, from_y, top, bottom
    )[0]
    return out.reshape((4 * rows,) + x.shape[1:])


def scatter_blocks(x):
    place = lax.axis_index("seq")
    rows, columns = x.shape[0] // 4, x.shape[1]
    half = rows // 2
    parts = x.reshape(4, 2, half, columns)

    def block(toward, which):
        return lax.dynamic_slice(
            parts, (lax.bitwise_xor(place, toward), which, 0, 0), (1, 1, half, columns)
        )[0, 0]

    sends = [jnp.stack([block(1, 0), block(3, 0)]), jnp.stack([block(2, 1), block(3, 1)])]
    return sends, [block(0, 0), block(0, 1)], [block(2, 0), block(1, 1)]


def scatter_begin(sends, kept, passed):
    mine, onward = [], []
    for sent, keep, hand, bit in zip(sends, kept, passed, (1, 2)):
        away = flip(sent, bit).astype(jnp.float32)
        mine.append(keep.astype(jnp.float32) + away[0])
        onward.append((hand.astype(jnp.float32) + away[1]).astype(jnp.bfloat16))
    return mine, onward


def scatter_end(mine, onward):
    last = flip(onward[1], 1)
    arrived = [tie(flip(onward[0], 2), last), last]
    return jnp.concatenate([a + b.astype(jnp.float32) for a, b in zip(mine, arrived)], axis=0)


def exchange_plane(x):
    place = lax.axis_index("seq")
    arrived = [pick(x, place)] + [
        flip(pick(x, lax.bitwise_xor(place, bit)), bit) for bit in (1, 2, 3)
    ]
    stacked = jnp.stack(arrived)
    return jnp.stack([pick(stacked, lax.bitwise_xor(place, j)) for j in range(4)])


def sum_chips(x):
    x = x + swap_cores(x)
    x = x + flip(x, 1)
    return x + flip(x, 2)


def sum_column(x):
    peers = lax.axis_size("dp")
    step = 1
    while step < peers:
        x = x + lax.ppermute(x, "dp", [(i, i ^ step) for i in range(peers)])
        step *= 2
    return x


def spread_tracks(x):
    rows = x.shape[0]
    lower = lax.axis_index("species") == 0
    human = jnp.pad(x, ((0, 0), (0, 12 * BLOCK - x.shape[1]))).reshape(rows, 4, 3, BLOCK)
    human = human.transpose(1, 2, 0, 3)
    mouse = x[:, : 4 * BLOCK].reshape(rows, 4, BLOCK).transpose(1, 0, 2)
    other = to_upper_core(human[:, 2])
    first = jnp.where(lower, human[:, 0], other)
    second = jnp.where(lower, human[:, 1], mouse)
    return jnp.concatenate([first, second], axis=-1)


def collect_tracks(x, tracks):
    rows = x.shape[1]
    lower = lax.axis_index("species") == 0
    other = to_lower_core(x[:, :, :BLOCK])
    human = jnp.stack([x[:, :, :BLOCK], x[:, :, BLOCK:], other], axis=1)
    human = human.transpose(2, 0, 1, 3).reshape(rows, 12 * BLOCK)[:, :tracks]
    mouse = x[:, :, BLOCK:].transpose(1, 0, 2).reshape(rows, 4 * BLOCK)
    mouse = jnp.pad(mouse, ((0, 0), (0, tracks - 4 * BLOCK)))
    return jnp.where(lower, human, mouse)


def layer_norm(value_entries, gain, shift):
    centre = jnp.mean(value_entries, axis=-1, keepdims=True)
    centred = value_entries - centre
    spread = jnp.mean(centred * centred, axis=-1, keepdims=True)
    return centred * lax.rsqrt(spread + EPSILON) * gain + shift


def gelu_and_slope(pre):
    act, back = jax.vjp(jax.nn.gelu, pre)
    return act.astype(jnp.bfloat16), back(jnp.ones_like(pre))[0].astype(jnp.bfloat16)


def dense(left, right):
    return jnp.dot(left, right, preferred_element_type=jnp.float32)


def dense_back(left, right):
    return lax.dot_general(
        left, right, (((1,), (1,)), ((), ())), preferred_element_type=jnp.float32
    )


def outer_sum(left, right):
    return lax.dot_general(
        left, right, (((0,), (0,)), ((), ())), preferred_element_type=jnp.float32
    )


def row_sum(value_entries):
    return jnp.sum(value_entries.astype(jnp.float32), axis=0)


def on_device(
    inputs,
    crop_start,
    rel_bucket,
    conv_weight,
    query_weight,
    key_weight,
    value_weight,
    out_weight,
    up_weight,
    down_weight,
    point_weight,
    rel_table,
    bn_gain,
    bn_shift,
    conv_bias,
    attn_gain,
    attn_shift,
    ffn_gain,
    ffn_shift,
    up_bias,
    down_bias,
    point_bias,
    head_weight,
    pred_grad,
):
    low = jnp.bfloat16
    wide = jnp.float32
    bin_count, chans = inputs.shape[2], inputs.shape[3]
    tracks = head_weight.shape[2]
    crop_rows = 4 * pred_grad.shape[2]
    seq_pos = lax.axis_index("seq")
    species_id = lax.axis_index("species")
    lower = species_id == 0
    dp_count = lax.axis_size("dp")
    device_count = 2 * dp_count * 4
    portion_index = lax.axis_index(EVERYWHERE)
    full_len = 4 * bin_count
    element_count = float(device_count * bin_count)
    half_width = WIDTH // 2

    outputs = chans // 4
    conv_share = exchange_plane(
        conv_weight.reshape(conv_weight.shape[0], 4, outputs).transpose(1, 0, 2)
    )
    conv_half = lax.all_gather(conv_share, "dp")

    value_entries = inputs[0, 0].astype(wide)
    small = (
        bn_gain, bn_shift, conv_bias, attn_gain, attn_shift, ffn_gain, ffn_shift, up_bias, down_bias,
        point_bias, rel_table,
    )

    def placed(x):
        whole = jnp.zeros((device_count * x.shape[0],), wide)
        return lax.dynamic_update_slice_in_dim(whole, x.astype(wide), portion_index * x.shape[0], 0)

    joined = jnp.concatenate(
        [jnp.sum(value_entries, axis=0), jnp.sum(value_entries * value_entries, axis=0)]
        + [placed(x) for x in small]
    )
    joined = sum_chips(joined.reshape(-1, 128))
    spread = spread_tracks(
        tie(jnp.concatenate([head_weight[0], pred_grad[0, 0]], axis=0), joined)
    )
    joined = sum_column(joined)
    joined = joined.reshape(-1)
    moment_one, moment_two = joined[:chans], joined[chans : 2 * chans]
    at = 2 * chans
    whole_small = []
    for x in small:
        size = device_count * x.shape[0]
        whole_small.append(joined[at : at + size])
        at += size
    (
        batchnorm_gain, batchnorm_shift, bias_conv, gain_attn, shift_attn, gain_ffn, shift_ffn, bias_up,
        bias_down, bias_point, table_flat,
    ) = whole_small

    pairs = HEADS // 2
    mixer_shard = jnp.concatenate(
        [
            x[:, h * width : (h + 1) * width]
            for h in range(pairs)
            for x, width in ((key_weight, 2 * QK), (value_weight, 2 * V))
        ]
        + [query_weight, out_weight],
        axis=1,
    )
    mixer_column = lax.all_gather(tie(mixer_shard, conv_share), "dp")
    depth = up_weight.shape[0]
    rest_shard = jnp.concatenate(
        [up_weight, down_weight[:depth], down_weight[depth:], point_weight], axis=1
    )
    rest_column = lax.all_gather(tie(rest_shard, mixer_column), "dp")
    head_rows = head_weight.shape[1]
    spread = exchange_plane(spread)
    track_grad = spread[:, head_rows:].reshape(crop_rows, 2 * BLOCK)
    kv_width, q_width, hidden = pairs * PAIR, query_weight.shape[1], up_weight.shape[1]
    ways = ((1, 2), (2, 1))

    def first_step(column, begin, size, *after):
        return [
            beside(tie(column[..., begin + i * size : begin + (i + 1) * size], *after), way[0])
            for i, way in enumerate(ways)
        ]

    def second_step(nears, *after):
        return [flip(tie(near, *after), way[1]) for near, way in zip(nears, ways)]

    def parts(nears, fars):
        return [(near, far) + way for near, far, way in zip(nears, fars, ways)]

    channel_average = moment_one / element_count
    inverse_deviation = lax.rsqrt(
        moment_two / element_count - channel_average * channel_average + EPSILON
    )
    standardized_input = (value_entries - channel_average) * inverse_deviation
    normed_rows = standardized_input * batchnorm_gain + batchnorm_shift
    activity, act_slope = gelu_and_slope(normed_rows)
    act_rows = gather_begin(activity)
    act_rows = act_rows[:3] + tuple(tie(x, spread) for x in act_rows[3:])
    act_all = gather_end(*act_rows)
    w_conv = both_halves(conv_half).reshape(WIDTH, chans, outputs)
    mixer_near = first_step(mixer_column, 0, mixer_column.shape[-1] // 2, act_all)
    mixer_far = second_step(mixer_near)
    conv_slice = conv_forward(act_all, w_conv).reshape(4, bin_count, outputs)
    w_head = lax.all_gather(tie(spread[:, :head_rows], rest_column), "dp").reshape(-1, 2 * BLOCK)
    conv_slice = exchange_plane(conv_slice)
    conv_out = bias_conv + conv_slice.transpose(1, 0, 2).reshape(bin_count, chans).astype(wide)
    first_sum = value_entries + conv_out
    w_kv, w_query, w_out = sorted_rows(
        parts(mixer_near, mixer_far),
        [
            (1, kv_width, [(0, kv_width, 0, 0)]),
            (1, q_width, [(kv_width, q_width, 0, 0)]),
            (1, chans, [(kv_width + q_width, chans, 0, 0)]),
        ],
    )
    normed_one = layer_norm(first_sum, gain_attn, shift_attn).astype(low)
    scale = QK ** (-0.5)
    kv_rows = gather_begin(dense(normed_one, w_kv).astype(low))
    query_rows = (dense(normed_one, w_query).astype(low).astype(wide) * scale).astype(low)
    ffn_near = first_step(rest_column, 0, hidden, *kv_rows[1:3])
    kv_all = gather_end(*kv_rows)
    ffn_far = second_step(ffn_near, kv_all)
    point_near = first_step(rest_column, 2 * hidden, point_weight.shape[1] // 2, kv_all)
    point_far = second_step(point_near, *ffn_far)
    bucket_window = lax.dynamic_slice_in_dim(
        jnp.pad(rel_bucket, (1, 0), constant_values=-1),
        full_len - bin_count - seq_pos * bin_count,
        full_len + bin_count,
    )
    window_onehot = (bucket_window[:, None] == jnp.arange(NB)[None, :]).astype(wide)
    distance_bias = lax.dot_general(
        table_flat.reshape(HEADS, NB), window_onehot, (((1,), (1,)), ((), ())),
        precision=lax.Precision.HIGHEST, preferred_element_type=wide,
    ).reshape(pairs, 2, full_len + bin_count)
    mixed = attn_fwd(query_rows, kv_all, distance_bias)
    second_sum = first_sum + dense(mixed, w_out)
    (w_up, w_down) = sorted_rows(
        parts(ffn_near, ffn_far),
        [
            (1, hidden, [(0, hidden, 0, 0)]),
            (2, chans, [(hidden, chans, 0, 0), (hidden + chans, chans, 1, 0)]),
        ],
    )
    normed_two = layer_norm(second_sum, gain_ffn, shift_ffn).astype(low)
    up_pre = dense(normed_two, w_up) + bias_up
    up_act, up_slope = gelu_and_slope(up_pre)
    third_sum = second_sum + dense(up_act, w_down) + bias_down
    third_rows = gather_begin(tie(third_sum.astype(low), w_head))
    third_all = gather_end(*third_rows)
    (w_point,) = sorted_rows(
        parts(point_near, point_far),
        [(1, point_weight.shape[1], [(0, point_weight.shape[1], 0, 0)])],
    )
    crop_at = crop_start[0, 0]
    cropped = lax.dynamic_slice_in_dim(third_all, crop_at, crop_rows, 0)
    point_pre = dense(cropped, w_point) + bias_point
    point_act, point_slope = gelu_and_slope(point_pre)

    human_act = jnp.where(lower, point_act, to_upper_core(point_act))
    column = jnp.arange(BLOCK)
    first_valid = 3 * BLOCK * seq_pos + jnp.where(lower, 0, 2 * BLOCK) + column < tracks
    second_valid = jnp.where(
        lower, 3 * BLOCK * seq_pos + BLOCK + column < tracks, BLOCK * seq_pos + column < TRK_M
    )
    preds, logit_grads = [], []
    for which, act, valid in ((0, human_act, first_valid), (1, point_act, second_valid)):
        span = slice(which * BLOCK, (which + 1) * BLOCK)
        mask = valid.astype(wide)
        logits = dense(act, w_head[:, span])
        preds.append((jax.nn.softplus(logits) * mask).astype(low))
        logit_grads.append(
            (track_grad[:, span].astype(wide) * mask * jax.nn.sigmoid(logits)).astype(low)
        )
    arrived = to_lower_core(dense_back(logit_grads[0], w_head[:, :BLOCK]).astype(low))
    logit_grad = jnp.concatenate(logit_grads, axis=1)
    own_grad = jnp.concatenate(
        [jnp.where(lower, logit_grads[0], jnp.zeros_like(logit_grads[0])), logit_grads[1]], axis=1
    )
    point_act_grad = dense_back(own_grad, w_head) + jnp.where(lower, arrived.astype(wide), 0.0)

    point_grad = (point_slope.astype(wide) * point_act_grad).astype(low)
    crop_grad = dense_back(point_grad, w_point).astype(low)
    third_blocks = scatter_blocks(place_rows(crop_grad, crop_at, full_len))
    third_mine, third_onward = scatter_begin(*third_blocks)
    head_part = tracks_grad(human_act, point_act, tie(logit_grad, *third_blocks[0])).reshape(
        dp_count, -1, 2 * BLOCK
    )
    point_grad = tie(point_grad, *third_blocks[0])
    point_sent = outer_half(cropped, point_grad, 1)
    point_other = swap_cores(point_sent)
    third_onward = [tie(x, head_part, point_sent) for x in third_onward]
    head_sum = lax.psum_scatter(head_part, "dp", scatter_dimension=0, tiled=False)
    grad_point_b = row_sum(point_grad)
    point_half = by_device(outer_half(cropped, point_grad, 0, point_other))
    third_grad = tie(scatter_end(third_mine, third_onward), point_half)

    preds = exchange_plane(
        tie(jnp.concatenate(preds, axis=1), third_grad).reshape(4, crop_rows // 4, 2 * BLOCK)
    )
    point_once = fold_both(point_half, 0)
    down_grad = third_grad.astype(low)
    down_other = swap_cores(outer_half(up_act, down_grad, 1))
    grad_down_b = row_sum(down_grad)
    up_grad = (up_slope.astype(wide) * dense_back(down_grad, w_down)).astype(low)
    down_half = by_device(outer_half(up_act, down_grad, 0, down_other))
    up_grad = tie(up_grad, down_half, *point_once)

    point_twice = fold_both(point_once, 1)
    down_once = fold_both(down_half, 0)
    up_other = swap_cores(outer_half(normed_two, up_grad, 1))
    grad_up_b = row_sum(up_grad)
    _, norm_two_back = jax.vjp(layer_norm, second_sum, gain_ffn, shift_ffn)
    second_part, grad_ffn_gain, grad_ffn_shift = norm_two_back(dense_back(up_grad, w_up))
    second_grad = third_grad + second_part
    out_grad = second_grad.astype(low)
    mixed_grad = dense_back(out_grad, w_out).astype(low)
    up_half = by_device(outer_half(normed_two, up_grad, 0, up_other))
    mixed_grad = tie(mixed_grad, up_half, *point_twice, *down_once)

    down_twice = fold_both(down_once, 1)
    up_once = fold_both(up_half, 0)
    out_other = swap_cores(outer_half(mixed, out_grad, 1))
    query_low, kv_part, distance_grad = attn_bwd(
        query_rows, kv_all, distance_bias, mixed_grad
    )
    kv_part = tie(kv_part, out_other, *down_twice, *up_once)

    up_twice = fold_both(up_once, 1)
    kv_mine, kv_onward = scatter_begin(*scatter_blocks(kv_part))
    grad_table = jnp.dot(
        distance_grad.reshape(HEADS, -1), window_onehot, precision=lax.Precision.HIGHEST,
        preferred_element_type=wide,
    ).reshape(HEADS * NB)
    out_half = by_device(outer_half(mixed, out_grad, 0, out_other))
    kv_onward = [tie(x, out_half, head_sum, *up_twice) for x in kv_onward]
    rest_sum = lax.psum_scatter(
        jnp.concatenate(
            [*point_twice, *up_twice]
            + [x[:, rows] for rows in (slice(0, depth), slice(depth, None)) for x in down_twice],
            axis=-1,
        ),
        "dp", scatter_dimension=0, tiled=False,
    ).astype(wide)
    kv_low = scatter_end(kv_mine, kv_onward).astype(low)

    mixer_grads = jnp.concatenate([kv_low, query_low], axis=1)
    mixer_other = swap_cores(outer_half(normed_one, mixer_grads, 1))
    normed_one_grad = dense_back(kv_low, w_kv) + dense_back(query_low, w_query)
    _, norm_one_back = jax.vjp(layer_norm, first_sum, gain_attn, shift_attn)
    first_part, grad_attn_gain, grad_attn_shift = norm_one_back(normed_one_grad)
    first_grad = second_grad + first_part
    mixer_half = jnp.concatenate(
        [by_device(outer_half(normed_one, mixer_grads, 0, mixer_other)), out_half], axis=-1
    )
    conv_grad = tie(first_grad.astype(low), mixer_half)
    grad_conv_b = row_sum(conv_grad)
    conv_part = exchange_plane(
        conv_grad.reshape(bin_count, 4, outputs).transpose(1, 0, 2)
    ).reshape(full_len, outputs)

    mixer_once = fold_both(mixer_half, 0)
    padded = jnp.pad(conv_part, ((half_width, half_width), (0, 0)))
    taps = jnp.concatenate(
        [padded[2 * half_width - k : 2 * half_width - k + full_len] for k in range(WIDTH)], axis=1
    )
    conv_sent = outer_half(act_all, taps, 1, taps=WIDTH)
    conv_other = swap_cores(conv_sent)
    act_part = conv_back(tie(taps, conv_sent), w_conv)
    conv_sum = outer_half(act_all, tie(taps, act_part), 0, conv_other, taps=WIDTH)
    act_part = tie(act_part, *mixer_once)
    mixer_twice = fold_both(mixer_once, 1)
    act_mine, act_onward = scatter_begin(*scatter_blocks(act_part))
    act_onward = [tie(x, *mixer_twice) for x in act_onward]
    act_grad = scatter_end(act_mine, act_onward)
    predictions = collect_tracks(tie(preds, *act_onward), tracks)
    grad_mixer = lax.psum_scatter(
        jnp.concatenate(mixer_twice, axis=-1), "dp", scatter_dimension=0, tiled=False
    ).astype(wide)
    conv_sum = lax.psum_scatter(
        conv_sum.reshape(dp_count, -1, outputs), "dp", scatter_dimension=0, tiled=False
    )
    grad_conv_w = exchange_plane(conv_sum.reshape(4, -1, outputs))
    grad_conv_w = grad_conv_w.transpose(1, 0, 2).reshape(-1, chans).astype(wide)
    head_grad = collect_tracks(
        exchange_plane(tie(head_sum, *act_onward).reshape(4, head_rows, 2 * BLOCK)), tracks
    ).astype(wide)
    grad_point_w = rest_sum[:, : point_weight.shape[1]]
    at = point_weight.shape[1]
    grad_up_w = rest_sum[:, at : at + hidden]
    at += hidden
    grad_down_w = jnp.concatenate([rest_sum[:, at : at + chans], rest_sum[:, at + chans :]], axis=0)
    normed_rows_gradient = act_slope.astype(wide) * act_grad
    vectors = (
        jnp.sum(normed_rows_gradient * standardized_input, axis=0),
        jnp.sum(normed_rows_gradient, axis=0),
        grad_table,
        grad_conv_b,
        grad_attn_gain,
        grad_attn_shift,
        grad_ffn_gain,
        grad_ffn_shift,
        grad_up_b,
        grad_down_b,
        grad_point_b,
    )
    summed = sum_column(sum_chips(jnp.concatenate(vectors).reshape(-1, 128))).reshape(-1)
    standardized_sum, plain_gradient_sum = summed[:chans], summed[chans : 2 * chans]
    input_grad = first_grad + batchnorm_gain * inverse_deviation * (
        normed_rows_gradient
        - plain_gradient_sum / element_count
        - standardized_input * standardized_sum / element_count
    )
    shares = []
    at = 0
    for x in vectors:
        size = x.shape[0] // device_count
        shares.append(lax.dynamic_slice_in_dim(summed, at + portion_index * size, size))
        at += x.shape[0]
    bn_gain_share, bn_shift_share, table_share, conv_b_share = shares[:4]
    attn_gain_share, attn_shift_share, ffn_gain_share, ffn_shift_share = shares[4:8]
    up_b_share, down_b_share, point_b_share = shares[8:]
    kv_share = grad_mixer[:, :kv_width].reshape(-1, pairs, PAIR)
    key_share = kv_share[:, :, : 2 * QK].reshape(-1, key_weight.shape[1])
    value_share = kv_share[:, :, 2 * QK :].reshape(-1, value_weight.shape[1])
    query_share = grad_mixer[:, kv_width : kv_width + q_width]
    out_share = grad_mixer[:, kv_width + q_width :]
    return (
        predictions[None, None],
        input_grad[None, None],
        grad_conv_w,
        query_share,
        key_share,
        value_share,
        out_share,
        grad_up_w,
        grad_down_w,
        grad_point_w,
        table_share,
        bn_gain_share,
        bn_shift_share,
        conv_b_share,
        attn_gain_share,
        attn_shift_share,
        ffn_gain_share,
        ffn_shift_share,
        up_b_share,
        down_b_share,
        point_b_share,
        head_grad[None],
    )


def solution(mesh):
    everywhere = P(EVERYWHERE)
    rows = P(EVERYWHERE, None)
    bins = P("species", "dp", "seq", None)
    head = P("species", ("dp", "seq"), None)
    return jax.shard_map(
        on_device,
        mesh=mesh,
        in_specs=(bins, P("species", "dp"), P()) + (rows,) * 8 + (everywhere,) * 11 + (head, bins),
        out_specs=(bins, bins) + (rows,) * 8 + (everywhere,) * 11 + (head,),
        check_vma=False,
    )
```

```python
import functools

import jax
import jax.numpy as jnp
from jax import lax
from jax.experimental import pallas as pl
from jax.experimental.pallas import tpu as pltpu
from jax.sharding import PartitionSpec as P

HEADS = 8
QK = 64
V = 192
TRK_M = 1643
WIDTH = 5
NB = 32
EPSILON = 1e-05
ROWS = 128
BLOCK = 512
TILE = 256
EVERYWHERE = ("species", "dp", "seq")


def _head_lanes(e):
    lane = lax.broadcasted_iota(jnp.int32, (1, 2 * QK), 1)
    return (lane >= QK) == (e == 1)

def _toeplitz(u):
    wide = jnp.broadcast_to(u, (ROWS, u.shape[-1]))
    return pltpu.roll(wide, 0, 1, stride=1, stride_axis=0)

def _soft(q, k, bias):
    s = lax.dot_general(q, k, (((1,), (1,)), ((), ())), preferred_element_type=jnp.float32) + bias
    e = jnp.exp(s - jnp.max(s, axis=-1, keepdims=True))
    return e * (1.0 / jnp.sum(e, axis=-1, keepdims=True))

def _join(first, second):
    lane = lax.broadcasted_iota(jnp.int32, (1, 128), 1)
    return jnp.concatenate([first[:, :128], jnp.where(lane < 64, first[:, 128:], second[:, :128]), second[:, 128:]], axis=1)

def attn_fwd_kernel(q_ref, kv_ref, u_ref, o_ref):
    rows = q_ref.shape[0]
    length = kv_ref.shape[0]
    k = kv_ref[:, : 2 * QK]
    tables = [_toeplitz(u_ref[0, e : e + 1, :]) for e in range(2)]
    for a in range(rows // ROWS):
        at = rows - ROWS * a
        span = slice(ROWS * a, ROWS * (a + 1))
        q = q_ref[span, :]
        outs = []
        for e in range(2):
            qe = jnp.where(_head_lanes(e), q, jnp.zeros_like(q))
            p = _soft(qe, k, tables[e][:, at : at + length]).astype(jnp.bfloat16)
            outs.append(jnp.dot(p, kv_ref[:, 128 * e + 128 : 128 * e + 384], preferred_element_type=jnp.float32))
        o_ref[span, :] = _join(*outs).astype(o_ref.dtype)

PAIR = 2 * QK + 2 * V


def attn_fwd(q, kv, u):
    rows, length = q.shape[0], kv.shape[0]
    pairs = q.shape[1] // (2 * QK)
    return pl.pallas_call(
        attn_fwd_kernel,
        grid=(pairs,),
        in_specs=[
            pl.BlockSpec((rows, 2 * QK), lambda h: (0, h)),
            pl.BlockSpec((length, PAIR), lambda h: (0, h)),
            pl.BlockSpec((1, 2, u.shape[-1]), lambda h: (h, 0, 0)),
        ],
        out_specs=pl.BlockSpec((rows, 2 * V), lambda h: (0, h)),
        out_shape=jax.ShapeDtypeStruct((rows, pairs * 2 * V), jnp.bfloat16),
        compiler_params=pltpu.CompilerParams(vmem_limit_bytes=48 * 2**20),
        cost_estimate=pl.CostEstimate(
            flops=14_000_000_000, bytes_accessed=0, transcendentals=0
        ),
        name="attention_forward",
    )(q, kv, u)


def attn_bwd_kernel(
    q_ref, kv_ref, u_ref, g_ref, dq_ref, dkv_ref, du_ref, p_scr, s_scr, d_scr
):
    rows = q_ref.shape[0]
    length = kv_ref.shape[0]
    k = kv_ref[:, : 2 * QK]
    lane2 = lax.broadcasted_iota(jnp.int32, (1, 256), 1)
    dqs, dks, dvs = [], [], []
    for e in range(2):
        table = _toeplitz(u_ref[0, e : e + 1, :])
        d_scr[...] = jnp.zeros_like(d_scr)
        keep = (lane2 < 192) if e == 0 else (lane2 >= 64)
        vcols = slice(128 * e, 128 * e + 256)
        for a in range(rows // ROWS):
            at = rows - ROWS * a
            span = slice(ROWS * a, ROWS * (a + 1))
            q = q_ref[span, :]
            qe = jnp.where(_head_lanes(e), q, jnp.zeros_like(q))
            p = _soft(qe, k, table[:, at : at + length])
            g = g_ref[span, vcols]
            g = jnp.where(keep, g, jnp.zeros_like(g))
            dp = lax.dot_general(g, kv_ref[:, 128 * e + 128 : 128 * e + 384], (((1,), (1,)), ((), ())), preferred_element_type=jnp.float32)
            ds = p * (dp - jnp.sum(p * dp, axis=-1, keepdims=True))
            p_scr[span, :] = p.astype(jnp.bfloat16)
            s_scr[span, :] = ds.astype(jnp.bfloat16)
            d_scr[:, at : at + length] += ds
        ds = s_scr[...]
        dqs.append(jnp.dot(ds, k, preferred_element_type=jnp.float32))
        dks.append(lax.dot_general(ds, q_ref[...], (((0,), (0,)), ((), ())), preferred_element_type=jnp.float32))
        dvs.append(lax.dot_general(p_scr[...], g_ref[:, vcols], (((0,), (0,)), ((), ())), preferred_element_type=jnp.float32))
        fold = d_scr[...]
        width = fold.shape[1]
        step = ROWS // 2
        while step:
            fold = fold[:step] + pltpu.roll(fold[step:], width - step, 1)
            step //= 2
        du_ref[0, e : e + 1, :] = fold
    lane = lax.broadcasted_iota(jnp.int32, (1, 128), 1)
    dq_ref[...] = (jnp.where(lane < QK, dqs[0], dqs[1]) * QK ** (-0.5)).astype(dq_ref.dtype)
    dkv_ref[:, : 2 * QK] = jnp.where(lane < QK, dks[0], dks[1]).astype(dkv_ref.dtype)
    dkv_ref[:, 2 * QK :] = _join(*dvs).astype(dkv_ref.dtype)

def attn_bwd(q, kv, u, g):
    rows, length = q.shape[0], kv.shape[0]
    pairs = q.shape[1] // (2 * QK)
    specs = [
        pl.BlockSpec((rows, 2 * QK), lambda h: (0, h)),
        pl.BlockSpec((length, PAIR), lambda h: (0, h)),
        pl.BlockSpec((1, 2, u.shape[-1]), lambda h: (h, 0, 0)),
    ]
    return pl.pallas_call(
        attn_bwd_kernel,
        grid=(pairs,),
        in_specs=specs + [pl.BlockSpec((rows, 2 * V), lambda h: (0, h))],
        out_specs=specs,
        out_shape=[
            jax.ShapeDtypeStruct(q.shape, jnp.bfloat16),
            jax.ShapeDtypeStruct(kv.shape, jnp.bfloat16),
            jax.ShapeDtypeStruct(u.shape, jnp.float32),
        ],
        scratch_shapes=[
            pltpu.VMEM((rows, length), jnp.bfloat16),
            pltpu.VMEM((rows, length), jnp.bfloat16),
            pltpu.VMEM((ROWS, u.shape[-1]), jnp.float32),
        ],
        compiler_params=pltpu.CompilerParams(vmem_limit_bytes=56 * 2**20),
        cost_estimate=pl.CostEstimate(
            flops=32_000_000_000, bytes_accessed=0, transcendentals=0
        ),
        name="attention_backward",
    )(q, kv, u, g)


def flip(x, bit):
    peers = lax.axis_size("seq")
    return lax.ppermute(x, "seq", [(i, i ^ bit) for i in range(peers)])


def swap_cores(x):
    return lax.ppermute(x, "species", [(0, 1), (1, 0)])


def to_upper_core(x):
    return lax.ppermute(x, "species", [(0, 1)])


def to_lower_core(x):
    return lax.ppermute(x, "species", [(1, 0)])


def pick(x, index, axis=0):
    return lax.dynamic_index_in_dim(x, index, axis, keepdims=False)


def sort_copies(moves, out_shapes, *pieces):
    def kernel(*refs):
        ins, refs = refs[: len(pieces)], refs[len(pieces) :]
        outs, refs = refs[: len(out_shapes)], refs[len(out_shapes) :]
        stages, (in_sems, out_sems) = refs[: len(out_shapes)], refs[len(out_shapes) :]
        place = {axis: lax.axis_index(axis) for axis in EVERYWHERE}
        arrivals, departures = [], []
        for i, (piece, source, array, target) in enumerate(moves(place)):
            stage = stages[array].at[target]
            arrivals.append(pltpu.make_async_copy(ins[piece].at[source], stage, in_sems.at[i]))
            departures.append(
                pltpu.make_async_copy(stage, outs[array].at[target], out_sems.at[i])
            )
        for copy in arrivals:
            copy.start()
        for arrival, departure in zip(arrivals, departures):
            arrival.wait()
            departure.start()
        for copy in departures:
            copy.wait()

    count = len(moves({axis: 0 for axis in EVERYWHERE}))
    held = sum(x.size * 4 for x in out_shapes) // 2
    return pl.pallas_call(
        kernel,
        in_specs=[pl.BlockSpec(memory_space=pl.ANY)] * len(pieces),
        out_specs=[pl.BlockSpec(memory_space=pl.ANY)] * len(out_shapes),
        out_shape=out_shapes,
        scratch_shapes=[pltpu.VMEM(x.shape, x.dtype) for x in out_shapes]
        + [pltpu.SemaphoreType.DMA((count,))] * 2,
        compiler_params=pltpu.CompilerParams(vmem_limit_bytes=held * 2 + 4 * 2**20),
        cost_estimate=pl.CostEstimate(flops=0, bytes_accessed=held * 4, transcendentals=0),
        name="sort_copies",
    )(*pieces)


def tie_kernel(*refs):
    del refs


def tie(x, *others):
    if not others:
        return x
    return pl.pallas_call(
        tie_kernel,
        in_specs=[pl.BlockSpec(memory_space=pl.ANY)] * (1 + len(others)),
        out_specs=pl.BlockSpec(memory_space=pl.ANY),
        out_shape=jax.ShapeDtypeStruct(x.shape, x.dtype),
        input_output_aliases={0: 0},
        cost_estimate=pl.CostEstimate(flops=0, bytes_accessed=0, transcendentals=0),
        name="tie",
    )(x, *others)


def beside(column, bit):
    return jnp.stack([column, flip(column, bit)])


def sorted_rows(parts, arrays):
    pieces = []
    for near, far, _, _ in parts:
        pieces += [near, far, swap_cores(near), swap_cores(far)]
    peers, depth = parts[0][0].shape[1:3]

    def moves(place):
        mine, seq = place["species"], place["seq"]
        everything = slice(None)
        found = []
        left = 0
        for part, (near, _, first, second) in enumerate(parts):
            right = left + near.shape[-1]
            runs = []
            for array, (_, _, blocks) in enumerate(arrays):
                for begin, size, which, column in blocks:
                    low, high = max(begin, left), min(begin + size, right)
                    if low < high:
                        source = pl.ds(low - left, high - low)
                        target = pl.ds(column + low - begin, high - low)
                        runs.append((array, source, which, target))
            left = right
            for piece, core, turn in (
                (0, mine, 0), (1, mine, second), (2, 1 - mine, 0), (3, 1 - mine, second)
            ):
                for m, bit in ((0, 0), (1, first)):
                    home = seq ^ (turn ^ bit)
                    for array, source, which, target in runs:
                        found.append(
                            (
                                4 * part + piece,
                                (m, everything, everything, source),
                                array,
                                (core, everything, home, which, everything, target),
                            )
                        )
        return found

    outs = sort_copies(
        moves,
        [
            jax.ShapeDtypeStruct((2, peers, 4, count, depth, width), pieces[0].dtype)
            for count, width, _ in arrays
        ],
        *pieces,
    )
    return [out.reshape(-1, out.shape[-1]) for out in outs]


def place_rows_kernel(at_ref, x_ref, o_ref, padded):
    rows, length, columns = x_ref.shape[0], o_ref.shape[0], o_ref.shape[1]
    margin = length - rows
    padded[...] = jnp.zeros_like(padded)
    padded[margin : margin + rows, :] = x_ref[...].astype(jnp.float32)
    begin = margin - at_ref[0]
    step = lax.rem(begin, 8)
    window = padded[pl.ds(pl.multiple_of(begin - step, 8), length + 8), :]
    turned = pltpu.roll(window.reshape(length // 8 + 1, 8, columns), lax.rem(8 - step, 8), 1)
    row = lax.broadcasted_iota(jnp.int32, (1, 8, columns), 1)
    placed = jnp.where(row < 8 - step, turned[:-1], turned[1:])
    o_ref[...] = placed.reshape(length, columns).astype(o_ref.dtype)


def place_rows(x, at, length):
    rows, columns = x.shape
    wide = 256
    return pl.pallas_call(
        place_rows_kernel,
        grid=(columns // wide,),
        in_specs=[
            pl.BlockSpec(memory_space=pltpu.SMEM),
            pl.BlockSpec((rows, wide), lambda i: (0, i)),
        ],
        out_specs=pl.BlockSpec((length, wide), lambda i: (0, i)),
        out_shape=jax.ShapeDtypeStruct((length, columns), x.dtype),
        scratch_shapes=[pltpu.VMEM((2 * length - rows + 8, wide), jnp.float32)],
        compiler_params=pltpu.CompilerParams(vmem_limit_bytes=32 * 2**20),
        name="place_rows",
    )(at.reshape(1), x)


def both_halves(mine):
    other = swap_cores(mine)

    def moves(place):
        core = place["species"]
        return [(0, (slice(None),), 0, (core,)), (1, (slice(None),), 0, (1 - core,))]

    return sort_copies(moves, [jax.ShapeDtypeStruct((2,) + mine.shape, mine.dtype)], mine, other)[0]


def tracks_grad_kernel(first_ref, second_ref, g_ref, o_ref):
    for which, left in enumerate((first_ref, second_ref)):
        span = slice(which * BLOCK, (which + 1) * BLOCK)
        o_ref[:, span] = lax.dot_general(
            left[...], g_ref[:, span], (((0,), (0,)), ((), ())), preferred_element_type=jnp.float32
        ).astype(o_ref.dtype)


def tracks_grad(first, second, g):
    rows, hidden = first.shape
    return pl.pallas_call(
        tracks_grad_kernel,
        grid=(hidden // TILE,),
        in_specs=[
            pl.BlockSpec((rows, TILE), lambda i: (0, i)),
            pl.BlockSpec((rows, TILE), lambda i: (0, i)),
            pl.BlockSpec((rows, 2 * BLOCK), lambda i: (0, 0)),
        ],
        out_specs=pl.BlockSpec((TILE, 2 * BLOCK), lambda i: (i, 0)),
        out_shape=jax.ShapeDtypeStruct((hidden, 2 * BLOCK), jnp.bfloat16),
        compiler_params=pltpu.CompilerParams(vmem_limit_bytes=32 * 2**20),
        cost_estimate=pl.CostEstimate(flops=4 * rows * hidden * 2 * BLOCK, bytes_accessed=0, transcendentals=0),
        name="tracks_grad",
    )(first, second, g)


def conv_forward_kernel(x_ref, w_ref, o_ref, total):
    length = x_ref.shape[0]
    margin = 8
    total[...] = jnp.zeros_like(total)
    for tap in range(WIDTH):
        for begin in range(0, length, TILE):
            product = jnp.dot(
                x_ref[begin : begin + TILE, :], w_ref[tap], preferred_element_type=jnp.float32
            )
            at = margin + begin + WIDTH // 2 - tap
            total[at : at + TILE, :] += product
    o_ref[...] = total[margin : margin + length, :].astype(o_ref.dtype)


def conv_forward(x, w):
    length, outputs = x.shape[0], w.shape[2]
    return pl.pallas_call(
        conv_forward_kernel,
        out_shape=jax.ShapeDtypeStruct((length, outputs), jnp.bfloat16),
        in_specs=[pl.BlockSpec(memory_space=pltpu.VMEM)] * 2,
        out_specs=pl.BlockSpec(memory_space=pltpu.VMEM),
        scratch_shapes=[pltpu.VMEM((length + 16, outputs), jnp.float32)],
        compiler_params=pltpu.CompilerParams(vmem_limit_bytes=40 * 2**20),
        cost_estimate=pl.CostEstimate(flops=3 * length * w.size, bytes_accessed=0, transcendentals=0),
        name="conv_forward",
    )(x, w)


def conv_back_kernel(g_ref, w_ref, o_ref):
    outputs = w_ref.shape[2]
    total = None
    for tap in range(WIDTH):
        term = lax.dot_general(
            g_ref[:, tap * outputs : (tap + 1) * outputs],
            w_ref[tap],
            (((1,), (1,)), ((), ())),
            preferred_element_type=jnp.float32,
        )
        total = term if total is None else total + term
    o_ref[...] = total.astype(o_ref.dtype)


def conv_back(g, w):
    length, chans = g.shape[0], w.shape[1]
    return pl.pallas_call(
        conv_back_kernel,
        grid=(length // TILE,),
        in_specs=[
            pl.BlockSpec((TILE, g.shape[1]), lambda i: (i, 0)),
            pl.BlockSpec(w.shape, lambda i: (0, 0, 0)),
        ],
        out_specs=pl.BlockSpec((TILE, chans), lambda i: (i, 0)),
        out_shape=jax.ShapeDtypeStruct((length, chans), jnp.bfloat16),
        compiler_params=pltpu.CompilerParams(vmem_limit_bytes=40 * 2**20),
        cost_estimate=pl.CostEstimate(flops=3 * length * w.size, bytes_accessed=0, transcendentals=0),
        name="conv_back",
    )(g, w)


def outer_kernel(base_ref, left_ref, right_ref, *refs):
    total = lax.dot_general(
        left_ref[...], right_ref[...], (((0,), (0,)), ((), ())), preferred_element_type=jnp.float32
    )
    if len(refs) == 2:
        total = total + refs[0][...].astype(jnp.float32)
    refs[-1][...] = total.astype(refs[-1].dtype)


def outer_half(left, right, which, more=None, taps=1):
    rows, chans = left.shape
    columns = right.shape[1] // taps
    tiles = chans // TILE
    count = taps * tiles // 2
    base = ((lax.axis_index("species") ^ which) * count).reshape(1).astype(jnp.int32)
    out_spec = pl.BlockSpec((TILE, columns), lambda i, at: (i, 0))
    return pl.pallas_call(
        outer_kernel,
        grid_spec=pltpu.PrefetchScalarGridSpec(
            num_scalar_prefetch=1,
            grid=(count,),
            in_specs=[
                pl.BlockSpec((rows, TILE), lambda i, at: (0, lax.rem(at[0] + i, tiles))),
                pl.BlockSpec((rows, columns), lambda i, at: (0, lax.div(at[0] + i, tiles))),
            ]
            + ([] if more is None else [out_spec]),
            out_specs=out_spec,
        ),
        out_shape=jax.ShapeDtypeStruct((count * TILE, columns), jnp.bfloat16),
        compiler_params=pltpu.CompilerParams(vmem_limit_bytes=40 * 2**20),
        cost_estimate=pl.CostEstimate(flops=3 * rows * count * TILE * columns, bytes_accessed=0, transcendentals=0),
        name="outer_half",
    )(base, left, right, *([] if more is None else [more]))


def by_device(total):
    peers = lax.axis_size("dp")
    return total.reshape(peers, 2, 2, total.shape[0] // (4 * peers), total.shape[1])


def fold(half, bit, after=()):
    axis = 2 if bit == 1 and half.ndim == 5 else 1
    here = lax.rem(lax.div(lax.axis_index("seq"), bit), 2)
    away = tie(flip(pick(half, 1 - here, axis), bit), *after)
    return (pick(half, here, axis).astype(jnp.float32) + away.astype(jnp.float32)).astype(half.dtype)


def fold_both(grads, steps, after=()):
    if steps == 0:
        middle = grads.shape[-1] // 2
        return fold(grads[..., :middle], 1, after), fold(grads[..., middle:], 2, after)
    return fold(grads[0], 2, after), fold(grads[1], 1, after)


def gather_begin(x):
    half = x.shape[0] // 2
    from_x, from_y = flip(x, 1), flip(x, 2)
    return x, from_x, from_y, from_x[:half], from_y[half:]


def gather_end(x, from_x, from_y, top, bottom):
    rows = x.shape[0]
    half = rows // 2
    top, bottom = flip(top, 2), flip(bottom, 1)

    def moves(place):
        seq = place["seq"]
        everything = slice(None)
        return [
            (0, (everything,), 0, (seq,)),
            (1, (everything,), 0, (seq ^ 1,)),
            (2, (everything,), 0, (seq ^ 2,)),
            (3, (everything,), 0, (seq ^ 3, pl.ds(0, half))),
            (4, (everything,), 0, (seq ^ 3, pl.ds(half, half))),
        ]

    out = sort_copies(
        moves, [jax.ShapeDtypeStruct((4,) + x.shape, x.dtype)], x, from_x, from_y, top, bottom
    )[0]
    return out.reshape((4 * rows,) + x.shape[1:])


def scatter_blocks(x):
    place = lax.axis_index("seq")
    rows, columns = x.shape[0] // 4, x.shape[1]
    half = rows // 2
    parts = x.reshape(4, 2, half, columns)

    def block(toward, which):
        return lax.dynamic_slice(
            parts, (lax.bitwise_xor(place, toward), which, 0, 0), (1, 1, half, columns)
        )[0, 0]

    sends = [jnp.stack([block(1, 0), block(3, 0)]), jnp.stack([block(2, 1), block(3, 1)])]
    return sends, [block(0, 0), block(0, 1)], [block(2, 0), block(1, 1)]


def scatter_begin(sends, kept, passed):
    mine, onward = [], []
    for sent, keep, hand, bit in zip(sends, kept, passed, (1, 2)):
        away = flip(sent, bit).astype(jnp.float32)
        mine.append(keep.astype(jnp.float32) + away[0])
        onward.append((hand.astype(jnp.float32) + away[1]).astype(jnp.bfloat16))
    return mine, onward


def scatter_end(mine, onward):
    last = flip(onward[1], 1)
    arrived = [tie(flip(onward[0], 2), last), last]
    return jnp.concatenate([a + b.astype(jnp.float32) for a, b in zip(mine, arrived)], axis=0)


def exchange_plane(x, after=()):
    place = lax.axis_index("seq")
    arrived = [pick(x, place)] + [
        tie(flip(pick(x, lax.bitwise_xor(place, bit)), bit), *after) for bit in (1, 2, 3)
    ]
    stacked = jnp.stack(arrived)
    return jnp.stack([pick(stacked, lax.bitwise_xor(place, j)) for j in range(4)])


def sum_chips(x):
    x = x + swap_cores(x)
    x = x + flip(x, 1)
    return x + flip(x, 2)


def sum_column(x):
    peers = lax.axis_size("dp")
    step = 1
    while step < peers:
        x = x + lax.ppermute(x, "dp", [(i, i ^ step) for i in range(peers)])
        step *= 2
    return x


def cut_tracks_kernel(steps, upper_ref, lower_ref, sent_ref, human_ref, mouse_ref):
    x = jnp.where(pl.program_id(0) < steps, upper_ref[...], lower_ref[...])
    tracks = x.shape[1]

    def columns(block):
        begin = block * BLOCK
        end = min(begin + BLOCK, tracks)
        if end <= begin:
            return jnp.zeros((x.shape[0], BLOCK), x.dtype)
        part = x[:, begin:end]
        if end < begin + BLOCK:
            part = jnp.concatenate(
                [part, jnp.zeros((x.shape[0], begin + BLOCK - end), x.dtype)], axis=1
            )
        return part

    for chip in range(4):
        human_ref[chip] = jnp.concatenate([columns(3 * chip), columns(3 * chip + 1)], axis=1)
        sent_ref[chip] = columns(3 * chip + 2)
        mouse_ref[chip] = columns(chip)


def spread_tracks(upper, lower):
    step = 16
    steps, more = upper.shape[0] // step, lower.shape[0] // step
    rows, tracks = upper.shape[0] + lower.shape[0], upper.shape[1]
    specs = [
        pl.BlockSpec((4, step, width), lambda i: (0, i, 0)) for width in (BLOCK, 2 * BLOCK, BLOCK)
    ]
    sent, human, mouse = pl.pallas_call(
        functools.partial(cut_tracks_kernel, steps),
        grid=(steps + more,),
        in_specs=[
            pl.BlockSpec((step, tracks), lambda i: (jnp.minimum(i, steps - 1), 0)),
            pl.BlockSpec((step, tracks), lambda i: (jnp.maximum(i - steps, 0), 0)),
        ],
        out_specs=specs,
        out_shape=[
            jax.ShapeDtypeStruct((4, rows, width), upper.dtype) for width in (BLOCK, 2 * BLOCK, BLOCK)
        ],
        compiler_params=pltpu.CompilerParams(vmem_limit_bytes=32 * 2**20),
        cost_estimate=pl.CostEstimate(flops=0, bytes_accessed=0, transcendentals=0),
        name="cut_tracks",
    )(upper, lower)
    other = to_upper_core(sent)
    return jnp.where(
        lax.axis_index("species") == 0, human, jnp.concatenate([other, mouse], axis=-1)
    )


def join_tracks_kernel(core_ref, x_ref, other_ref, o_ref):
    tracks = o_ref.shape[1]

    def put(block, value):
        begin = block * BLOCK
        width = min(BLOCK, tracks - begin)
        if width > 0:
            o_ref[:, begin : begin + width] = value[:, :width].astype(o_ref.dtype)

    @pl.when(core_ref[0] == 0)
    def _():
        for chip in range(4):
            put(3 * chip, x_ref[chip, :, :BLOCK])
            put(3 * chip + 1, x_ref[chip, :, BLOCK:])
            put(3 * chip + 2, other_ref[chip])

    @pl.when(core_ref[0] != 0)
    def _():
        o_ref[...] = jnp.zeros_like(o_ref)
        for chip in range(4):
            put(chip, x_ref[chip, :, BLOCK:])


def collect_tracks(x, tracks, dtype):
    rows, step = x.shape[1], 16
    other = to_lower_core(x[:, :, :BLOCK])
    return pl.pallas_call(
        join_tracks_kernel,
        grid=(rows // step,),
        in_specs=[
            pl.BlockSpec(memory_space=pltpu.SMEM),
            pl.BlockSpec((4, step, 2 * BLOCK), lambda i: (0, i, 0)),
            pl.BlockSpec((4, step, BLOCK), lambda i: (0, i, 0)),
        ],
        out_specs=pl.BlockSpec((step, tracks), lambda i: (i, 0)),
        out_shape=jax.ShapeDtypeStruct((rows, tracks), dtype),
        compiler_params=pltpu.CompilerParams(vmem_limit_bytes=32 * 2**20),
        cost_estimate=pl.CostEstimate(flops=0, bytes_accessed=0, transcendentals=0),
        name="join_tracks",
    )(lax.axis_index("species").reshape(1).astype(jnp.int32), x, other)


def layer_norm(value_entries, gain, shift):
    centre = jnp.mean(value_entries, axis=-1, keepdims=True)
    centred = value_entries - centre
    spread = jnp.mean(centred * centred, axis=-1, keepdims=True)
    return centred * lax.rsqrt(spread + EPSILON) * gain + shift


def gelu_and_slope(pre):
    act, back = jax.vjp(jax.nn.gelu, pre)
    return act.astype(jnp.bfloat16), back(jnp.ones_like(pre))[0].astype(jnp.bfloat16)


def dense(left, right):
    return jnp.dot(left, right, preferred_element_type=jnp.float32)


def dense_back(left, right):
    return lax.dot_general(
        left, right, (((1,), (1,)), ((), ())), preferred_element_type=jnp.float32
    )


def outer_sum(left, right):
    return lax.dot_general(
        left, right, (((0,), (0,)), ((), ())), preferred_element_type=jnp.float32
    )


def row_sum(value_entries):
    return jnp.sum(value_entries.astype(jnp.float32), axis=0)


def on_device(
    inputs,
    crop_start,
    rel_bucket,
    conv_weight,
    query_weight,
    key_weight,
    value_weight,
    out_weight,
    up_weight,
    down_weight,
    point_weight,
    rel_table,
    bn_gain,
    bn_shift,
    conv_bias,
    attn_gain,
    attn_shift,
    ffn_gain,
    ffn_shift,
    up_bias,
    down_bias,
    point_bias,
    head_weight,
    pred_grad,
):
    low = jnp.bfloat16
    wide = jnp.float32
    bin_count, chans = inputs.shape[2], inputs.shape[3]
    tracks = head_weight.shape[2]
    crop_rows = 4 * pred_grad.shape[2]
    seq_pos = lax.axis_index("seq")
    species_id = lax.axis_index("species")
    lower = species_id == 0
    dp_count = lax.axis_size("dp")
    device_count = 2 * dp_count * 4
    portion_index = lax.axis_index(EVERYWHERE)
    full_len = 4 * bin_count
    element_count = float(device_count * bin_count)
    half_width = WIDTH // 2

    outputs = chans // 4
    conv_share = exchange_plane(
        conv_weight.reshape(conv_weight.shape[0], 4, outputs).transpose(1, 0, 2)
    )
    conv_half = lax.all_gather(conv_share, "dp")

    value_entries = inputs[0, 0].astype(wide)
    small = (
        bn_gain, bn_shift, conv_bias, attn_gain, attn_shift, ffn_gain, ffn_shift, up_bias, down_bias,
        point_bias, rel_table,
    )

    def placed(x):
        whole = jnp.zeros((device_count * x.shape[0],), wide)
        return lax.dynamic_update_slice_in_dim(whole, x.astype(wide), portion_index * x.shape[0], 0)

    joined = jnp.concatenate(
        [jnp.sum(value_entries, axis=0), jnp.sum(value_entries * value_entries, axis=0)]
        + [placed(x) for x in small]
    )
    joined = sum_chips(joined.reshape(-1, 128))
    spread = spread_tracks(head_weight[0], pred_grad[0, 0])
    joined = sum_column(joined)
    joined = joined.reshape(-1)
    moment_one, moment_two = joined[:chans], joined[chans : 2 * chans]
    at = 2 * chans
    whole_small = []
    for x in small:
        size = device_count * x.shape[0]
        whole_small.append(joined[at : at + size])
        at += size
    (
        batchnorm_gain, batchnorm_shift, bias_conv, gain_attn, shift_attn, gain_ffn, shift_ffn, bias_up,
        bias_down, bias_point, table_flat,
    ) = whole_small

    pairs = HEADS // 2
    mixer_shard = jnp.concatenate(
        [
            x[:, h * width : (h + 1) * width]
            for h in range(pairs)
            for x, width in ((key_weight, 2 * QK), (value_weight, 2 * V))
        ]
        + [query_weight, out_weight],
        axis=1,
    )
    mixer_column = lax.all_gather(tie(mixer_shard, conv_share), "dp")
    depth = up_weight.shape[0]
    rest_shard = jnp.concatenate(
        [up_weight, down_weight[:depth], down_weight[depth:], point_weight], axis=1
    )
    rest_column = lax.all_gather(tie(rest_shard, mixer_column), "dp")
    head_rows = head_weight.shape[1]
    kv_width, q_width, hidden = pairs * PAIR, query_weight.shape[1], up_weight.shape[1]
    ways = ((1, 2), (2, 1))

    def first_step(column, begin, size, *after):
        return [
            beside(tie(column[..., begin + i * size : begin + (i + 1) * size], *after), way[0])
            for i, way in enumerate(ways)
        ]

    def second_step(nears, *after):
        nears[:] = [tie(near, *after) for near in nears]
        return [flip(near, way[1]) for near, way in zip(nears, ways)]

    def parts(nears, fars):
        return [(near, far) + way for near, far, way in zip(nears, fars, ways)]

    channel_average = moment_one / element_count
    inverse_deviation = lax.rsqrt(
        moment_two / element_count - channel_average * channel_average + EPSILON
    )
    standardized_input = (value_entries - channel_average) * inverse_deviation
    normed_rows = standardized_input * batchnorm_gain + batchnorm_shift
    activity, act_slope = gelu_and_slope(normed_rows)
    act_rows = gather_begin(activity)
    act_all = gather_end(*act_rows)
    w_conv = both_halves(tie(conv_half, *act_rows[1:3])).reshape(WIDTH, chans, outputs)
    mixer_column = tie(mixer_column, w_conv)
    mixer_near = first_step(mixer_column, 0, mixer_column.shape[-1] // 2)
    conv_slice = conv_forward(act_all, w_conv).reshape(4, bin_count, outputs)
    spread = exchange_plane(spread, (conv_slice,))
    track_grad = spread[:, head_rows:].reshape(crop_rows, 2 * BLOCK)
    mixer_far = second_step(mixer_near, conv_slice)
    w_head = lax.all_gather(tie(spread[:, :head_rows], rest_column), "dp").reshape(-1, 2 * BLOCK)
    conv_slice = exchange_plane(conv_slice)
    conv_out = bias_conv + conv_slice.transpose(1, 0, 2).reshape(bin_count, chans).astype(wide)
    first_sum = value_entries + conv_out
    w_kv, w_query, w_out = sorted_rows(
        parts(mixer_near, mixer_far),
        [
            (1, kv_width, [(0, kv_width, 0, 0)]),
            (1, q_width, [(kv_width, q_width, 0, 0)]),
            (1, chans, [(kv_width + q_width, chans, 0, 0)]),
        ],
    )
    normed_one = layer_norm(first_sum, gain_attn, shift_attn).astype(low)
    scale = QK ** (-0.5)
    kv_rows = gather_begin(dense(normed_one, w_kv).astype(low))
    query_rows = (dense(normed_one, w_query).astype(low).astype(wide) * scale).astype(low)
    ffn_near = first_step(rest_column, 0, hidden, *kv_rows[1:3])
    point_near = first_step(rest_column, 2 * hidden, point_weight.shape[1] // 2, *kv_rows[1:3])
    kv_all = gather_end(*kv_rows)
    ffn_far = second_step(ffn_near, kv_all)
    point_far = second_step(point_near, *ffn_far)
    bucket_window = lax.dynamic_slice_in_dim(
        jnp.pad(rel_bucket, (1, 0), constant_values=-1),
        full_len - bin_count - seq_pos * bin_count,
        full_len + bin_count,
    )
    window_onehot = (bucket_window[:, None] == jnp.arange(NB)[None, :]).astype(wide)
    distance_bias = lax.dot_general(
        table_flat.reshape(HEADS, NB), window_onehot, (((1,), (1,)), ((), ())),
        precision=lax.Precision.HIGHEST, preferred_element_type=wide,
    ).reshape(pairs, 2, full_len + bin_count)
    mixed = attn_fwd(query_rows, kv_all, distance_bias)
    second_sum = first_sum + dense(mixed, w_out)
    ffn_far = [tie(x, second_sum) for x in ffn_far]
    (w_up, w_down) = sorted_rows(
        parts(ffn_near, ffn_far),
        [
            (1, hidden, [(0, hidden, 0, 0)]),
            (2, chans, [(hidden, chans, 0, 0), (hidden + chans, chans, 1, 0)]),
        ],
    )
    normed_two = layer_norm(second_sum, gain_ffn, shift_ffn).astype(low)
    up_pre = dense(normed_two, w_up) + bias_up
    up_act, up_slope = gelu_and_slope(up_pre)
    third_sum = second_sum + dense(up_act, w_down) + bias_down
    third_rows = gather_begin(tie(third_sum.astype(low), w_head))
    point_far = [tie(x, third_rows[0]) for x in point_far]
    third_all = gather_end(*third_rows)
    (w_point,) = sorted_rows(
        parts(point_near, point_far),
        [(1, point_weight.shape[1], [(0, point_weight.shape[1], 0, 0)])],
    )
    crop_at = crop_start[0, 0]
    cropped = lax.dynamic_slice_in_dim(third_all, crop_at, crop_rows, 0)
    point_pre = dense(cropped, w_point) + bias_point
    point_act, point_slope = gelu_and_slope(point_pre)

    human_act = jnp.where(lower, point_act, to_upper_core(point_act))
    column = jnp.arange(BLOCK)
    first_valid = 3 * BLOCK * seq_pos + jnp.where(lower, 0, 2 * BLOCK) + column < tracks
    second_valid = jnp.where(
        lower, 3 * BLOCK * seq_pos + BLOCK + column < tracks, BLOCK * seq_pos + column < TRK_M
    )
    preds, logit_grads = [], []
    for which, act, valid in ((0, human_act, first_valid), (1, point_act, second_valid)):
        span = slice(which * BLOCK, (which + 1) * BLOCK)
        mask = valid.astype(wide)
        logits = dense(act, w_head[:, span])
        preds.append((jax.nn.softplus(logits) * mask).astype(low))
        logit_grads.append(
            (track_grad[:, span].astype(wide) * mask * jax.nn.sigmoid(logits)).astype(low)
        )
    arrived = to_lower_core(dense_back(logit_grads[0], w_head[:, :BLOCK]).astype(low))
    logit_grad = jnp.concatenate(logit_grads, axis=1)
    own_grad = jnp.concatenate(
        [jnp.where(lower, logit_grads[0], jnp.zeros_like(logit_grads[0])), logit_grads[1]], axis=1
    )
    point_act_grad = dense_back(own_grad, w_head) + jnp.where(lower, arrived.astype(wide), 0.0)

    point_grad = (point_slope.astype(wide) * point_act_grad).astype(low)
    crop_grad = dense_back(point_grad, w_point).astype(low)
    third_blocks = scatter_blocks(place_rows(crop_grad, crop_at, full_len))
    third_mine, third_onward = scatter_begin(*third_blocks)
    head_part = tracks_grad(human_act, point_act, tie(logit_grad, *third_blocks[0])).reshape(
        dp_count, -1, 2 * BLOCK
    )
    point_grad = tie(point_grad, *third_blocks[0])
    point_sent = outer_half(cropped, point_grad, 1)
    point_other = swap_cores(point_sent)
    third_onward = [tie(x, head_part, point_sent) for x in third_onward]
    head_sum = lax.psum_scatter(head_part, "dp", scatter_dimension=0, tiled=False)
    grad_point_b = row_sum(point_grad)
    point_half = by_device(outer_half(cropped, point_grad, 0, point_other))
    third_grad = tie(scatter_end(third_mine, third_onward), point_half)

    preds = exchange_plane(
        tie(jnp.concatenate(preds, axis=1), third_grad).reshape(4, crop_rows // 4, 2 * BLOCK)
    )
    down_grad = third_grad.astype(low)
    down_other = swap_cores(outer_half(up_act, down_grad, 1))
    grad_down_b = row_sum(down_grad)
    up_grad = (up_slope.astype(wide) * dense_back(down_grad, w_down)).astype(low)
    point_once = fold_both(point_half, 0, (up_grad,))
    down_half = by_device(outer_half(up_act, down_grad, 0, down_other))
    up_grad = tie(up_grad, down_half)

    up_other = swap_cores(outer_half(normed_two, up_grad, 1))
    grad_up_b = row_sum(up_grad)
    _, norm_two_back = jax.vjp(layer_norm, second_sum, gain_ffn, shift_ffn)
    second_part, grad_ffn_gain, grad_ffn_shift = norm_two_back(dense_back(up_grad, w_up))
    second_grad = third_grad + second_part
    out_grad = second_grad.astype(low)
    mixed_grad = dense_back(out_grad, w_out).astype(low)
    up_half = by_device(outer_half(normed_two, up_grad, 0, up_other))
    mixed_grad = tie(mixed_grad, up_half, preds, *point_once)

    out_other = swap_cores(outer_half(mixed, out_grad, 1))
    query_low, kv_part, distance_grad = attn_bwd(
        query_rows, kv_all, distance_bias, mixed_grad
    )
    point_twice = fold_both(point_once, 1, (kv_part,))
    down_once = fold_both(down_half, 0, (kv_part,))
    kv_part = tie(kv_part, out_other, *point_twice, *down_once)

    kv_mine, kv_onward = scatter_begin(*scatter_blocks(kv_part))
    grad_table = jnp.dot(
        distance_grad.reshape(HEADS, -1), window_onehot, precision=lax.Precision.HIGHEST,
        preferred_element_type=wide,
    ).reshape(HEADS * NB)
    out_half = by_device(outer_half(mixed, out_grad, 0, out_other))
    kv_onward = [tie(x, out_half, head_sum) for x in kv_onward]
    kv_low = scatter_end(kv_mine, kv_onward).astype(low)

    mixer_grads = jnp.concatenate([kv_low, query_low], axis=1)
    mixer_sent = outer_half(normed_one, mixer_grads, 1)
    mixer_other = swap_cores(mixer_sent)
    down_twice = fold_both([tie(x, *kv_onward) for x in down_once], 1, (kv_low,))
    up_once = fold_both(tie(up_half, *kv_onward), 0, (mixer_sent,))
    normed_one_grad = dense_back(kv_low, w_kv) + dense_back(tie(query_low, mixer_sent), w_query)
    _, norm_one_back = jax.vjp(layer_norm, first_sum, gain_attn, shift_attn)
    first_part, grad_attn_gain, grad_attn_shift = norm_one_back(normed_one_grad)
    first_grad = second_grad + first_part
    conv_grad = first_grad.astype(low)
    grad_conv_b = row_sum(conv_grad)
    conv_part = exchange_plane(
        conv_grad.reshape(bin_count, 4, outputs).transpose(1, 0, 2)
    ).reshape(full_len, outputs)
    mixer_half = jnp.concatenate(
        [by_device(outer_half(normed_one, mixer_grads, 0, mixer_other)), out_half], axis=-1
    )
    up_twice = fold_both(up_once, 1, (conv_grad,))
    rest_sum = lax.psum_scatter(
        jnp.concatenate(
            [*point_twice, *up_twice]
            + [x[:, rows] for rows in (slice(0, depth), slice(depth, None)) for x in down_twice],
            axis=-1,
        ),
        "dp", scatter_dimension=0, tiled=False,
    ).astype(wide)
    conv_part = tie(conv_part, mixer_half, *up_twice)

    mixer_once = fold_both(mixer_half, 0)
    padded = jnp.pad(conv_part, ((half_width, half_width), (0, 0)))
    taps = jnp.concatenate(
        [padded[2 * half_width - k : 2 * half_width - k + full_len] for k in range(WIDTH)], axis=1
    )
    conv_sent = outer_half(act_all, taps, 1, taps=WIDTH)
    conv_other = swap_cores(conv_sent)
    act_part = conv_back(tie(taps, conv_sent), w_conv)
    conv_sum = outer_half(act_all, tie(taps, act_part), 0, conv_other, taps=WIDTH)
    act_part = tie(act_part, *mixer_once)
    mixer_twice = fold_both(mixer_once, 1)
    act_mine, act_onward = scatter_begin(*scatter_blocks(act_part))
    act_onward = [tie(x, *mixer_twice) for x in act_onward]
    act_grad = scatter_end(act_mine, act_onward)
    predictions = collect_tracks(tie(preds, *act_onward), tracks, low)
    grad_mixer = lax.psum_scatter(
        jnp.concatenate(mixer_twice, axis=-1), "dp", scatter_dimension=0, tiled=False
    ).astype(wide)
    conv_sum = lax.psum_scatter(
        conv_sum.reshape(dp_count, -1, outputs), "dp", scatter_dimension=0, tiled=False
    )
    grad_conv_w = exchange_plane(conv_sum.reshape(4, -1, outputs))
    grad_conv_w = grad_conv_w.transpose(1, 0, 2).reshape(-1, chans).astype(wide)
    head_grad = collect_tracks(
        exchange_plane(tie(head_sum, *act_onward).reshape(4, head_rows, 2 * BLOCK)), tracks, wide
    )
    grad_point_w = rest_sum[:, : point_weight.shape[1]]
    at = point_weight.shape[1]
    grad_up_w = rest_sum[:, at : at + hidden]
    at += hidden
    grad_down_w = jnp.concatenate([rest_sum[:, at : at + chans], rest_sum[:, at + chans :]], axis=0)
    normed_rows_gradient = act_slope.astype(wide) * act_grad
    vectors = (
        jnp.sum(normed_rows_gradient * standardized_input, axis=0),
        jnp.sum(normed_rows_gradient, axis=0),
        grad_table,
        grad_conv_b,
        grad_attn_gain,
        grad_attn_shift,
        grad_ffn_gain,
        grad_ffn_shift,
        grad_up_b,
        grad_down_b,
        grad_point_b,
    )
    summed = sum_column(sum_chips(jnp.concatenate(vectors).reshape(-1, 128))).reshape(-1)
    standardized_sum, plain_gradient_sum = summed[:chans], summed[chans : 2 * chans]
    input_grad = first_grad + batchnorm_gain * inverse_deviation * (
        normed_rows_gradient
        - plain_gradient_sum / element_count
        - standardized_input * standardized_sum / element_count
    )
    shares = []
    at = 0
    for x in vectors:
        size = x.shape[0] // device_count
        shares.append(lax.dynamic_slice_in_dim(summed, at + portion_index * size, size))
        at += x.shape[0]
    bn_gain_share, bn_shift_share, table_share, conv_b_share = shares[:4]
    attn_gain_share, attn_shift_share, ffn_gain_share, ffn_shift_share = shares[4:8]
    up_b_share, down_b_share, point_b_share = shares[8:]
    kv_share = grad_mixer[:, :kv_width].reshape(-1, pairs, PAIR)
    key_share = kv_share[:, :, : 2 * QK].reshape(-1, key_weight.shape[1])
    value_share = kv_share[:, :, 2 * QK :].reshape(-1, value_weight.shape[1])
    query_share = grad_mixer[:, kv_width : kv_width + q_width]
    out_share = grad_mixer[:, kv_width + q_width :]
    return (
        predictions[None, None],
        input_grad[None, None],
        grad_conv_w,
        query_share,
        key_share,
        value_share,
        out_share,
        grad_up_w,
        grad_down_w,
        grad_point_w,
        table_share,
        bn_gain_share,
        bn_shift_share,
        conv_b_share,
        attn_gain_share,
        attn_shift_share,
        ffn_gain_share,
        ffn_shift_share,
        up_b_share,
        down_b_share,
        point_b_share,
        head_grad[None],
    )


def solution(mesh):
    everywhere = P(EVERYWHERE)
    rows = P(EVERYWHERE, None)
    bins = P("species", "dp", "seq", None)
    head = P("species", ("dp", "seq"), None)
    return jax.shard_map(
        on_device,
        mesh=mesh,
        in_specs=(bins, P("species", "dp"), P()) + (rows,) * 8 + (everywhere,) * 11 + (head, bins),
        out_specs=(bins, bins) + (rows,) * 8 + (everywhere,) * 11 + (head,),
        check_vma=False,
    )
```

```python
import functools

import jax
import jax.numpy as jnp
from jax import lax
from jax.experimental import pallas as pl
from jax.experimental.pallas import tpu as pltpu
from jax.sharding import PartitionSpec as P

HEADS = 8
QK = 64
V = 192
TRK_M = 1643
WIDTH = 5
NB = 32
EPSILON = 1e-05
ROWS = 128
BLOCK = 512
TILE = 256
EVERYWHERE = ("species", "dp", "seq")


def _head_lanes(e):
    lane = lax.broadcasted_iota(jnp.int32, (1, 2 * QK), 1)
    return (lane >= QK) == (e == 1)

def _toeplitz(u):
    wide = jnp.broadcast_to(u, (ROWS, u.shape[-1]))
    return pltpu.roll(wide, 0, 1, stride=1, stride_axis=0)

def _soft(q, k, bias):
    s = lax.dot_general(q, k, (((1,), (1,)), ((), ())), preferred_element_type=jnp.float32) + bias
    e = jnp.exp(s - jnp.max(s, axis=-1, keepdims=True))
    return e * (1.0 / jnp.sum(e, axis=-1, keepdims=True))

def _join(first, second):
    lane = lax.broadcasted_iota(jnp.int32, (1, 128), 1)
    return jnp.concatenate([first[:, :128], jnp.where(lane < 64, first[:, 128:], second[:, :128]), second[:, 128:]], axis=1)

def attn_fwd_kernel(q_ref, kv_ref, u_ref, o_ref):
    rows = q_ref.shape[0]
    length = kv_ref.shape[0]
    k = kv_ref[:, : 2 * QK]
    tables = [_toeplitz(u_ref[0, e : e + 1, :]) for e in range(2)]
    for a in range(rows // ROWS):
        at = rows - ROWS * a
        span = slice(ROWS * a, ROWS * (a + 1))
        q = q_ref[span, :]
        outs = []
        for e in range(2):
            qe = jnp.where(_head_lanes(e), q, jnp.zeros_like(q))
            p = _soft(qe, k, tables[e][:, at : at + length]).astype(jnp.bfloat16)
            outs.append(jnp.dot(p, kv_ref[:, 128 * e + 128 : 128 * e + 384], preferred_element_type=jnp.float32))
        o_ref[span, :] = _join(*outs).astype(o_ref.dtype)

PAIR = 2 * QK + 2 * V


def attn_fwd(q, kv, u):
    rows, length = q.shape[0], kv.shape[0]
    pairs = q.shape[1] // (2 * QK)
    return pl.pallas_call(
        attn_fwd_kernel,
        grid=(pairs,),
        in_specs=[
            pl.BlockSpec((rows, 2 * QK), lambda h: (0, h)),
            pl.BlockSpec((length, PAIR), lambda h: (0, h)),
            pl.BlockSpec((1, 2, u.shape[-1]), lambda h: (h, 0, 0)),
        ],
        out_specs=pl.BlockSpec((rows, 2 * V), lambda h: (0, h)),
        out_shape=jax.ShapeDtypeStruct((rows, pairs * 2 * V), jnp.bfloat16),
        compiler_params=pltpu.CompilerParams(vmem_limit_bytes=48 * 2**20),
        cost_estimate=pl.CostEstimate(
            flops=14_000_000_000, bytes_accessed=0, transcendentals=0
        ),
        name="attention_forward",
    )(q, kv, u)


def attn_bwd_kernel(
    q_ref, kv_ref, u_ref, g_ref, dq_ref, dkv_ref, du_ref, p_scr, s_scr, d_scr
):
    rows = q_ref.shape[0]
    length = kv_ref.shape[0]
    k = kv_ref[:, : 2 * QK]
    lane2 = lax.broadcasted_iota(jnp.int32, (1, 256), 1)
    dqs, dks, dvs = [], [], []
    for e in range(2):
        table = _toeplitz(u_ref[0, e : e + 1, :])
        d_scr[...] = jnp.zeros_like(d_scr)
        keep = (lane2 < 192) if e == 0 else (lane2 >= 64)
        vcols = slice(128 * e, 128 * e + 256)
        for a in range(rows // ROWS):
            at = rows - ROWS * a
            span = slice(ROWS * a, ROWS * (a + 1))
            q = q_ref[span, :]
            qe = jnp.where(_head_lanes(e), q, jnp.zeros_like(q))
            p = _soft(qe, k, table[:, at : at + length])
            g = g_ref[span, vcols]
            g = jnp.where(keep, g, jnp.zeros_like(g))
            dp = lax.dot_general(g, kv_ref[:, 128 * e + 128 : 128 * e + 384], (((1,), (1,)), ((), ())), preferred_element_type=jnp.float32)
            ds = p * (dp - jnp.sum(p * dp, axis=-1, keepdims=True))
            p_scr[span, :] = p.astype(jnp.bfloat16)
            s_scr[span, :] = ds.astype(jnp.bfloat16)
            d_scr[:, at : at + length] += ds
        ds = s_scr[...]
        dqs.append(jnp.dot(ds, k, preferred_element_type=jnp.float32))
        dks.append(lax.dot_general(ds, q_ref[...], (((0,), (0,)), ((), ())), preferred_element_type=jnp.float32))
        dvs.append(lax.dot_general(p_scr[...], g_ref[:, vcols], (((0,), (0,)), ((), ())), preferred_element_type=jnp.float32))
        fold = d_scr[...]
        width = fold.shape[1]
        step = ROWS // 2
        while step:
            fold = fold[:step] + pltpu.roll(fold[step:], width - step, 1)
            step //= 2
        du_ref[0, e : e + 1, :] = fold
    lane = lax.broadcasted_iota(jnp.int32, (1, 128), 1)
    dq_ref[...] = (jnp.where(lane < QK, dqs[0], dqs[1]) * QK ** (-0.5)).astype(dq_ref.dtype)
    dkv_ref[:, : 2 * QK] = jnp.where(lane < QK, dks[0], dks[1]).astype(dkv_ref.dtype)
    dkv_ref[:, 2 * QK :] = _join(*dvs).astype(dkv_ref.dtype)

def attn_bwd(q, kv, u, g):
    rows, length = q.shape[0], kv.shape[0]
    pairs = q.shape[1] // (2 * QK)
    specs = [
        pl.BlockSpec((rows, 2 * QK), lambda h: (0, h)),
        pl.BlockSpec((length, PAIR), lambda h: (0, h)),
        pl.BlockSpec((1, 2, u.shape[-1]), lambda h: (h, 0, 0)),
    ]
    return pl.pallas_call(
        attn_bwd_kernel,
        grid=(pairs,),
        in_specs=specs + [pl.BlockSpec((rows, 2 * V), lambda h: (0, h))],
        out_specs=specs,
        out_shape=[
            jax.ShapeDtypeStruct(q.shape, jnp.bfloat16),
            jax.ShapeDtypeStruct(kv.shape, jnp.bfloat16),
            jax.ShapeDtypeStruct(u.shape, jnp.float32),
        ],
        scratch_shapes=[
            pltpu.VMEM((rows, length), jnp.bfloat16),
            pltpu.VMEM((rows, length), jnp.bfloat16),
            pltpu.VMEM((ROWS, u.shape[-1]), jnp.float32),
        ],
        compiler_params=pltpu.CompilerParams(vmem_limit_bytes=56 * 2**20),
        cost_estimate=pl.CostEstimate(
            flops=32_000_000_000, bytes_accessed=0, transcendentals=0
        ),
        name="attention_backward",
    )(q, kv, u, g)


def flip(x, bit):
    peers = lax.axis_size("seq")
    return lax.ppermute(x, "seq", [(i, i ^ bit) for i in range(peers)])


def swap_cores(x):
    return lax.ppermute(x, "species", [(0, 1), (1, 0)])


def to_upper_core(x):
    return lax.ppermute(x, "species", [(0, 1)])


def to_lower_core(x):
    return lax.ppermute(x, "species", [(1, 0)])


def pick(x, index, axis=0):
    return lax.dynamic_index_in_dim(x, index, axis, keepdims=False)


def sort_copies(moves, out_shapes, *pieces):
    def kernel(*refs):
        ins, refs = refs[: len(pieces)], refs[len(pieces) :]
        outs, refs = refs[: len(out_shapes)], refs[len(out_shapes) :]
        stages, (in_sems, out_sems) = refs[: len(out_shapes)], refs[len(out_shapes) :]
        place = {axis: lax.axis_index(axis) for axis in EVERYWHERE}
        arrivals, departures = [], []
        for i, (piece, source, array, target) in enumerate(moves(place)):
            stage = stages[array].at[target]
            arrivals.append(pltpu.make_async_copy(ins[piece].at[source], stage, in_sems.at[i]))
            departures.append(
                pltpu.make_async_copy(stage, outs[array].at[target], out_sems.at[i])
            )
        for copy in arrivals:
            copy.start()
        for arrival, departure in zip(arrivals, departures):
            arrival.wait()
            departure.start()
        for copy in departures:
            copy.wait()

    count = len(moves({axis: 0 for axis in EVERYWHERE}))
    held = sum(x.size * 4 for x in out_shapes) // 2
    return pl.pallas_call(
        kernel,
        in_specs=[pl.BlockSpec(memory_space=pl.ANY)] * len(pieces),
        out_specs=[pl.BlockSpec(memory_space=pl.ANY)] * len(out_shapes),
        out_shape=out_shapes,
        scratch_shapes=[pltpu.VMEM(x.shape, x.dtype) for x in out_shapes]
        + [pltpu.SemaphoreType.DMA((count,))] * 2,
        compiler_params=pltpu.CompilerParams(vmem_limit_bytes=held * 2 + 4 * 2**20),
        cost_estimate=pl.CostEstimate(flops=0, bytes_accessed=held * 4, transcendentals=0),
        name="sort_copies",
    )(*pieces)


def tie_kernel(*refs):
    del refs


def tie(x, *others):
    if not others:
        return x
    return pl.pallas_call(
        tie_kernel,
        in_specs=[pl.BlockSpec(memory_space=pl.ANY)] * (1 + len(others)),
        out_specs=pl.BlockSpec(memory_space=pl.ANY),
        out_shape=jax.ShapeDtypeStruct(x.shape, x.dtype),
        input_output_aliases={0: 0},
        cost_estimate=pl.CostEstimate(flops=0, bytes_accessed=0, transcendentals=0),
        name="tie",
    )(x, *others)


def beside(column, bit):
    return jnp.stack([column, flip(column, bit)])


def sorted_rows(parts, arrays):
    pieces = []
    for near, far, _, _ in parts:
        pieces += [near, far, swap_cores(near), swap_cores(far)]
    peers, depth = parts[0][0].shape[1:3]

    def moves(place):
        mine, seq = place["species"], place["seq"]
        everything = slice(None)
        found = []
        left = 0
        for part, (near, _, first, second) in enumerate(parts):
            right = left + near.shape[-1]
            runs = []
            for array, (_, _, blocks) in enumerate(arrays):
                for begin, size, which, column in blocks:
                    low, high = max(begin, left), min(begin + size, right)
                    if low < high:
                        source = pl.ds(low - left, high - low)
                        target = pl.ds(column + low - begin, high - low)
                        runs.append((array, source, which, target))
            left = right
            for piece, core, turn in (
                (0, mine, 0), (1, mine, second), (2, 1 - mine, 0), (3, 1 - mine, second)
            ):
                for m, bit in ((0, 0), (1, first)):
                    home = seq ^ (turn ^ bit)
                    for array, source, which, target in runs:
                        found.append(
                            (
                                4 * part + piece,
                                (m, everything, everything, source),
                                array,
                                (core, everything, home, which, everything, target),
                            )
                        )
        return found

    outs = sort_copies(
        moves,
        [
            jax.ShapeDtypeStruct((2, peers, 4, count, depth, width), pieces[0].dtype)
            for count, width, _ in arrays
        ],
        *pieces,
    )
    return [out.reshape(-1, out.shape[-1]) for out in outs]


def place_rows_kernel(at_ref, x_ref, o_ref, padded):
    rows, length, columns = x_ref.shape[0], o_ref.shape[0], o_ref.shape[1]
    margin = length - rows
    padded[...] = jnp.zeros_like(padded)
    padded[margin : margin + rows, :] = x_ref[...].astype(jnp.float32)
    begin = margin - at_ref[0]
    step = lax.rem(begin, 8)
    window = padded[pl.ds(pl.multiple_of(begin - step, 8), length + 8), :]
    turned = pltpu.roll(window.reshape(length // 8 + 1, 8, columns), lax.rem(8 - step, 8), 1)
    row = lax.broadcasted_iota(jnp.int32, (1, 8, columns), 1)
    placed = jnp.where(row < 8 - step, turned[:-1], turned[1:])
    o_ref[...] = placed.reshape(length, columns).astype(o_ref.dtype)


def place_rows(x, at, length):
    rows, columns = x.shape
    wide = 256
    return pl.pallas_call(
        place_rows_kernel,
        grid=(columns // wide,),
        in_specs=[
            pl.BlockSpec(memory_space=pltpu.SMEM),
            pl.BlockSpec((rows, wide), lambda i: (0, i)),
        ],
        out_specs=pl.BlockSpec((length, wide), lambda i: (0, i)),
        out_shape=jax.ShapeDtypeStruct((length, columns), x.dtype),
        scratch_shapes=[pltpu.VMEM((2 * length - rows + 8, wide), jnp.float32)],
        compiler_params=pltpu.CompilerParams(vmem_limit_bytes=32 * 2**20),
        name="place_rows",
    )(at.reshape(1), x)


def both_halves(mine):
    other = swap_cores(mine)

    def moves(place):
        core = place["species"]
        return [(0, (slice(None),), 0, (core,)), (1, (slice(None),), 0, (1 - core,))]

    return sort_copies(moves, [jax.ShapeDtypeStruct((2,) + mine.shape, mine.dtype)], mine, other)[0]


def tracks_grad_kernel(first_ref, second_ref, g_ref, o_ref):
    for which, left in enumerate((first_ref, second_ref)):
        span = slice(which * BLOCK, (which + 1) * BLOCK)
        o_ref[:, span] = lax.dot_general(
            left[...], g_ref[:, span], (((0,), (0,)), ((), ())), preferred_element_type=jnp.float32
        ).astype(o_ref.dtype)


def tracks_grad(first, second, g):
    rows, hidden = first.shape
    return pl.pallas_call(
        tracks_grad_kernel,
        grid=(hidden // TILE,),
        in_specs=[
            pl.BlockSpec((rows, TILE), lambda i: (0, i)),
            pl.BlockSpec((rows, TILE), lambda i: (0, i)),
            pl.BlockSpec((rows, 2 * BLOCK), lambda i: (0, 0)),
        ],
        out_specs=pl.BlockSpec((TILE, 2 * BLOCK), lambda i: (i, 0)),
        out_shape=jax.ShapeDtypeStruct((hidden, 2 * BLOCK), jnp.bfloat16),
        compiler_params=pltpu.CompilerParams(vmem_limit_bytes=32 * 2**20),
        cost_estimate=pl.CostEstimate(flops=4 * rows * hidden * 2 * BLOCK, bytes_accessed=0, transcendentals=0),
        name="tracks_grad",
    )(first, second, g)


def conv_forward_kernel(x_ref, w_ref, o_ref, total):
    length = x_ref.shape[0]
    margin = 8
    total[...] = jnp.zeros_like(total)
    for tap in range(WIDTH):
        for begin in range(0, length, TILE):
            product = jnp.dot(
                x_ref[begin : begin + TILE, :], w_ref[tap], preferred_element_type=jnp.float32
            )
            at = margin + begin + WIDTH // 2 - tap
            total[at : at + TILE, :] += product
    o_ref[...] = total[margin : margin + length, :].astype(o_ref.dtype)


def conv_forward(x, w):
    length, outputs = x.shape[0], w.shape[2]
    return pl.pallas_call(
        conv_forward_kernel,
        out_shape=jax.ShapeDtypeStruct((length, outputs), jnp.bfloat16),
        in_specs=[pl.BlockSpec(memory_space=pltpu.VMEM)] * 2,
        out_specs=pl.BlockSpec(memory_space=pltpu.VMEM),
        scratch_shapes=[pltpu.VMEM((length + 16, outputs), jnp.float32)],
        compiler_params=pltpu.CompilerParams(vmem_limit_bytes=40 * 2**20),
        cost_estimate=pl.CostEstimate(flops=3 * length * w.size, bytes_accessed=0, transcendentals=0),
        name="conv_forward",
    )(x, w)


def conv_back_kernel(g_ref, w_ref, o_ref):
    outputs = w_ref.shape[2]
    total = None
    for tap in range(WIDTH):
        term = lax.dot_general(
            g_ref[:, tap * outputs : (tap + 1) * outputs],
            w_ref[tap],
            (((1,), (1,)), ((), ())),
            preferred_element_type=jnp.float32,
        )
        total = term if total is None else total + term
    o_ref[...] = total.astype(o_ref.dtype)


def conv_back(g, w):
    length, chans = g.shape[0], w.shape[1]
    return pl.pallas_call(
        conv_back_kernel,
        grid=(length // TILE,),
        in_specs=[
            pl.BlockSpec((TILE, g.shape[1]), lambda i: (i, 0)),
            pl.BlockSpec(w.shape, lambda i: (0, 0, 0)),
        ],
        out_specs=pl.BlockSpec((TILE, chans), lambda i: (i, 0)),
        out_shape=jax.ShapeDtypeStruct((length, chans), jnp.bfloat16),
        compiler_params=pltpu.CompilerParams(vmem_limit_bytes=40 * 2**20),
        cost_estimate=pl.CostEstimate(flops=3 * length * w.size, bytes_accessed=0, transcendentals=0),
        name="conv_back",
    )(g, w)


def outer_kernel(base_ref, left_ref, right_ref, *refs):
    total = lax.dot_general(
        left_ref[...], right_ref[...], (((0,), (0,)), ((), ())), preferred_element_type=jnp.float32
    )
    if len(refs) == 2:
        total = total + refs[0][...].astype(jnp.float32)
    refs[-1][...] = total.astype(refs[-1].dtype)


def outer_half(left, right, which, more=None, taps=1):
    rows, chans = left.shape
    columns = right.shape[1] // taps
    tiles = chans // TILE
    count = taps * tiles // 2
    base = ((lax.axis_index("species") ^ which) * count).reshape(1).astype(jnp.int32)
    out_spec = pl.BlockSpec((TILE, columns), lambda i, at: (i, 0))
    return pl.pallas_call(
        outer_kernel,
        grid_spec=pltpu.PrefetchScalarGridSpec(
            num_scalar_prefetch=1,
            grid=(count,),
            in_specs=[
                pl.BlockSpec((rows, TILE), lambda i, at: (0, lax.rem(at[0] + i, tiles))),
                pl.BlockSpec((rows, columns), lambda i, at: (0, lax.div(at[0] + i, tiles))),
            ]
            + ([] if more is None else [out_spec]),
            out_specs=out_spec,
        ),
        out_shape=jax.ShapeDtypeStruct((count * TILE, columns), jnp.bfloat16),
        compiler_params=pltpu.CompilerParams(vmem_limit_bytes=40 * 2**20),
        cost_estimate=pl.CostEstimate(flops=3 * rows * count * TILE * columns, bytes_accessed=0, transcendentals=0),
        name="outer_half",
    )(base, left, right, *([] if more is None else [more]))


def by_device(total):
    peers = lax.axis_size("dp")
    return total.reshape(peers, 2, 2, total.shape[0] // (4 * peers), total.shape[1])


def fold(half, bit, after=()):
    axis = 2 if bit == 1 and half.ndim == 5 else 1
    here = lax.rem(lax.div(lax.axis_index("seq"), bit), 2)
    away = tie(flip(pick(half, 1 - here, axis), bit), *after)
    return (pick(half, here, axis).astype(jnp.float32) + away.astype(jnp.float32)).astype(half.dtype)


def fold_both(grads, steps, after=()):
    if steps == 0:
        middle = grads.shape[-1] // 2
        return fold(grads[..., :middle], 1, after), fold(grads[..., middle:], 2, after)
    return fold(grads[0], 2, after), fold(grads[1], 1, after)


def gather_begin(x):
    half = x.shape[0] // 2
    from_x, from_y = flip(x, 1), flip(x, 2)
    return x, from_x, from_y, from_x[:half], from_y[half:]


def gather_end(x, from_x, from_y, top, bottom):
    rows = x.shape[0]
    half = rows // 2
    top, bottom = flip(top, 2), flip(bottom, 1)

    def moves(place):
        seq = place["seq"]
        everything = slice(None)
        return [
            (0, (everything,), 0, (seq,)),
            (1, (everything,), 0, (seq ^ 1,)),
            (2, (everything,), 0, (seq ^ 2,)),
            (3, (everything,), 0, (seq ^ 3, pl.ds(0, half))),
            (4, (everything,), 0, (seq ^ 3, pl.ds(half, half))),
        ]

    out = sort_copies(
        moves, [jax.ShapeDtypeStruct((4,) + x.shape, x.dtype)], x, from_x, from_y, top, bottom
    )[0]
    return out.reshape((4 * rows,) + x.shape[1:])


def scatter_blocks(x):
    place = lax.axis_index("seq")
    rows, columns = x.shape[0] // 4, x.shape[1]
    half = rows // 2
    parts = x.reshape(4, 2, half, columns)

    def block(toward, which):
        return lax.dynamic_slice(
            parts, (lax.bitwise_xor(place, toward), which, 0, 0), (1, 1, half, columns)
        )[0, 0]

    sends = [jnp.stack([block(1, 0), block(3, 0)]), jnp.stack([block(2, 1), block(3, 1)])]
    return sends, [block(0, 0), block(0, 1)], [block(2, 0), block(1, 1)]


def scatter_begin(sends, kept, passed):
    mine, onward = [], []
    for sent, keep, hand, bit in zip(sends, kept, passed, (1, 2)):
        away = flip(sent, bit).astype(jnp.float32)
        mine.append(keep.astype(jnp.float32) + away[0])
        onward.append((hand.astype(jnp.float32) + away[1]).astype(jnp.bfloat16))
    return mine, onward


def scatter_end(mine, onward):
    last = flip(onward[1], 1)
    arrived = [tie(flip(onward[0], 2), last), last]
    return jnp.concatenate([a + b.astype(jnp.float32) for a, b in zip(mine, arrived)], axis=0)


def exchange_plane(x, after=()):
    place = lax.axis_index("seq")
    arrived = [pick(x, place)] + [
        tie(flip(pick(x, lax.bitwise_xor(place, bit)), bit), *after) for bit in (1, 2, 3)
    ]
    stacked = jnp.stack(arrived)
    return jnp.stack([pick(stacked, lax.bitwise_xor(place, j)) for j in range(4)])


def sum_chips(x):
    x = x + swap_cores(x)
    x = x + flip(x, 1)
    return x + flip(x, 2)


def sum_column(x):
    peers = lax.axis_size("dp")
    step = 1
    while step < peers:
        x = x + lax.ppermute(x, "dp", [(i, i ^ step) for i in range(peers)])
        step *= 2
    return x


def cut_tracks_kernel(steps, upper_ref, lower_ref, sent_ref, human_ref, mouse_ref):
    x = jnp.where(pl.program_id(0) < steps, upper_ref[...], lower_ref[...])
    tracks = x.shape[1]

    def columns(block):
        begin = block * BLOCK
        end = min(begin + BLOCK, tracks)
        if end <= begin:
            return jnp.zeros((x.shape[0], BLOCK), x.dtype)
        part = x[:, begin:end]
        if end < begin + BLOCK:
            part = jnp.concatenate(
                [part, jnp.zeros((x.shape[0], begin + BLOCK - end), x.dtype)], axis=1
            )
        return part

    for chip in range(4):
        human_ref[chip] = jnp.concatenate([columns(3 * chip), columns(3 * chip + 1)], axis=1)
        sent_ref[chip] = columns(3 * chip + 2)
        mouse_ref[chip] = columns(chip)


def spread_tracks(upper, lower):
    step = 16
    steps, more = upper.shape[0] // step, lower.shape[0] // step
    rows, tracks = upper.shape[0] + lower.shape[0], upper.shape[1]
    specs = [
        pl.BlockSpec((4, step, width), lambda i: (0, i, 0)) for width in (BLOCK, 2 * BLOCK, BLOCK)
    ]
    sent, human, mouse = pl.pallas_call(
        functools.partial(cut_tracks_kernel, steps),
        grid=(steps + more,),
        in_specs=[
            pl.BlockSpec((step, tracks), lambda i: (jnp.minimum(i, steps - 1), 0)),
            pl.BlockSpec((step, tracks), lambda i: (jnp.maximum(i - steps, 0), 0)),
        ],
        out_specs=specs,
        out_shape=[
            jax.ShapeDtypeStruct((4, rows, width), upper.dtype) for width in (BLOCK, 2 * BLOCK, BLOCK)
        ],
        compiler_params=pltpu.CompilerParams(vmem_limit_bytes=32 * 2**20),
        cost_estimate=pl.CostEstimate(flops=0, bytes_accessed=0, transcendentals=0),
        name="cut_tracks",
    )(upper, lower)
    other = to_upper_core(sent)
    return jnp.where(
        lax.axis_index("species") == 0, human, jnp.concatenate([other, mouse], axis=-1)
    )


def join_tracks_kernel(core_ref, x_ref, other_ref, o_ref):
    tracks = o_ref.shape[1]

    def put(block, value):
        begin = block * BLOCK
        width = min(BLOCK, tracks - begin)
        if width > 0:
            o_ref[:, begin : begin + width] = value[:, :width].astype(o_ref.dtype)

    @pl.when(core_ref[0] == 0)
    def _():
        for chip in range(4):
            put(3 * chip, x_ref[chip, :, :BLOCK])
            put(3 * chip + 1, x_ref[chip, :, BLOCK:])
            put(3 * chip + 2, other_ref[chip])

    @pl.when(core_ref[0] != 0)
    def _():
        o_ref[...] = jnp.zeros_like(o_ref)
        for chip in range(4):
            put(chip, x_ref[chip, :, BLOCK:])


def collect_tracks(x, tracks, dtype):
    rows, step = x.shape[1], 16
    other = to_lower_core(x[:, :, :BLOCK])
    return pl.pallas_call(
        join_tracks_kernel,
        grid=(rows // step,),
        in_specs=[
            pl.BlockSpec(memory_space=pltpu.SMEM),
            pl.BlockSpec((4, step, 2 * BLOCK), lambda i: (0, i, 0)),
            pl.BlockSpec((4, step, BLOCK), lambda i: (0, i, 0)),
        ],
        out_specs=pl.BlockSpec((step, tracks), lambda i: (i, 0)),
        out_shape=jax.ShapeDtypeStruct((rows, tracks), dtype),
        compiler_params=pltpu.CompilerParams(vmem_limit_bytes=32 * 2**20),
        cost_estimate=pl.CostEstimate(flops=0, bytes_accessed=0, transcendentals=0),
        name="join_tracks",
    )(lax.axis_index("species").reshape(1).astype(jnp.int32), x, other)


def layer_norm(value_entries, gain, shift):
    centre = jnp.mean(value_entries, axis=-1, keepdims=True)
    centred = value_entries - centre
    spread = jnp.mean(centred * centred, axis=-1, keepdims=True)
    return centred * lax.rsqrt(spread + EPSILON) * gain + shift


def gelu_and_slope(pre):
    act, back = jax.vjp(jax.nn.gelu, pre)
    return act.astype(jnp.bfloat16), back(jnp.ones_like(pre))[0].astype(jnp.bfloat16)


def dense(left, right):
    return jnp.dot(left, right, preferred_element_type=jnp.float32)


def dense_back(left, right):
    return lax.dot_general(
        left, right, (((1,), (1,)), ((), ())), preferred_element_type=jnp.float32
    )


def outer_sum(left, right):
    return lax.dot_general(
        left, right, (((0,), (0,)), ((), ())), preferred_element_type=jnp.float32
    )


def row_sum(value_entries):
    return jnp.sum(value_entries.astype(jnp.float32), axis=0)


def on_device(
    inputs,
    crop_start,
    rel_bucket,
    conv_weight,
    query_weight,
    key_weight,
    value_weight,
    out_weight,
    up_weight,
    down_weight,
    point_weight,
    rel_table,
    bn_gain,
    bn_shift,
    conv_bias,
    attn_gain,
    attn_shift,
    ffn_gain,
    ffn_shift,
    up_bias,
    down_bias,
    point_bias,
    head_weight,
    pred_grad,
):
    low = jnp.bfloat16
    wide = jnp.float32
    bin_count, chans = inputs.shape[2], inputs.shape[3]
    tracks = head_weight.shape[2]
    crop_rows = 4 * pred_grad.shape[2]
    seq_pos = lax.axis_index("seq")
    species_id = lax.axis_index("species")
    lower = species_id == 0
    dp_count = lax.axis_size("dp")
    device_count = 2 * dp_count * 4
    portion_index = lax.axis_index(EVERYWHERE)
    full_len = 4 * bin_count
    element_count = float(device_count * bin_count)
    half_width = WIDTH // 2

    outputs = chans // 4
    conv_share = exchange_plane(
        conv_weight.reshape(conv_weight.shape[0], 4, outputs).transpose(1, 0, 2)
    )
    conv_half = lax.all_gather(conv_share, "dp")

    value_entries = inputs[0, 0].astype(wide)
    small = (
        bn_gain, bn_shift, conv_bias, attn_gain, attn_shift, ffn_gain, ffn_shift, up_bias, down_bias,
        point_bias, rel_table,
    )

    def placed(x):
        whole = jnp.zeros((device_count * x.shape[0],), wide)
        return lax.dynamic_update_slice_in_dim(whole, x.astype(wide), portion_index * x.shape[0], 0)

    joined = jnp.concatenate(
        [jnp.sum(value_entries, axis=0), jnp.sum(value_entries * value_entries, axis=0)]
        + [placed(x) for x in small]
    )
    joined = sum_chips(joined.reshape(-1, 128))
    spread = spread_tracks(head_weight[0], pred_grad[0, 0])
    joined = sum_column(joined)
    joined = joined.reshape(-1)
    moment_one, moment_two = joined[:chans], joined[chans : 2 * chans]
    at = 2 * chans
    whole_small = []
    for x in small:
        size = device_count * x.shape[0]
        whole_small.append(joined[at : at + size])
        at += size
    (
        batchnorm_gain, batchnorm_shift, bias_conv, gain_attn, shift_attn, gain_ffn, shift_ffn, bias_up,
        bias_down, bias_point, table_flat,
    ) = whole_small

    pairs = HEADS // 2
    mixer_shard = jnp.concatenate(
        [
            x[:, h * width : (h + 1) * width]
            for h in range(pairs)
            for x, width in ((key_weight, 2 * QK), (value_weight, 2 * V))
        ]
        + [query_weight, out_weight],
        axis=1,
    )
    mixer_column = lax.all_gather(tie(mixer_shard, conv_share), "dp")
    depth = up_weight.shape[0]
    rest_shard = jnp.concatenate(
        [up_weight, down_weight[:depth], down_weight[depth:], point_weight], axis=1
    )
    rest_column = lax.all_gather(tie(rest_shard, mixer_column), "dp")
    head_rows = head_weight.shape[1]
    kv_width, q_width, hidden = pairs * PAIR, query_weight.shape[1], up_weight.shape[1]
    ways = ((1, 2), (2, 1))

    def first_step(column, begin, size, *after):
        return [
            beside(tie(column[..., begin + i * size : begin + (i + 1) * size], *after), way[0])
            for i, way in enumerate(ways)
        ]

    def second_step(nears, *after):
        nears[:] = [tie(near, *after) for near in nears]
        return [flip(near, way[1]) for near, way in zip(nears, ways)]

    def parts(nears, fars):
        return [(near, far) + way for near, far, way in zip(nears, fars, ways)]

    channel_average = moment_one / element_count
    inverse_deviation = lax.rsqrt(
        moment_two / element_count - channel_average * channel_average + EPSILON
    )
    standardized_input = (value_entries - channel_average) * inverse_deviation
    normed_rows = standardized_input * batchnorm_gain + batchnorm_shift
    activity, act_slope = gelu_and_slope(normed_rows)
    act_rows = gather_begin(activity)
    act_all = gather_end(*act_rows)
    w_conv = both_halves(tie(conv_half, *act_rows[1:3])).reshape(WIDTH, chans, outputs)
    mixer_column = tie(mixer_column, w_conv)
    mixer_near = first_step(mixer_column, 0, mixer_column.shape[-1] // 2)
    conv_slice = conv_forward(act_all, w_conv).reshape(4, bin_count, outputs)
    spread = exchange_plane(spread, (conv_slice,))
    track_grad = spread[:, head_rows:].reshape(crop_rows, 2 * BLOCK)
    mixer_far = second_step(mixer_near, conv_slice)
    w_head = lax.all_gather(tie(spread[:, :head_rows], rest_column), "dp").reshape(-1, 2 * BLOCK)
    conv_slice = exchange_plane(conv_slice)
    conv_out = bias_conv + conv_slice.transpose(1, 0, 2).reshape(bin_count, chans).astype(wide)
    first_sum = value_entries + conv_out
    w_kv, w_query, w_out = sorted_rows(
        parts(mixer_near, mixer_far),
        [
            (1, kv_width, [(0, kv_width, 0, 0)]),
            (1, q_width, [(kv_width, q_width, 0, 0)]),
            (1, chans, [(kv_width + q_width, chans, 0, 0)]),
        ],
    )
    normed_one = layer_norm(first_sum, gain_attn, shift_attn).astype(low)
    scale = QK ** (-0.5)
    kv_rows = gather_begin(dense(normed_one, w_kv).astype(low))
    query_rows = (dense(normed_one, w_query).astype(low).astype(wide) * scale).astype(low)
    ffn_near = first_step(rest_column, 0, hidden, *kv_rows[1:3])
    point_near = first_step(rest_column, 2 * hidden, point_weight.shape[1] // 2, *kv_rows[1:3])
    kv_all = gather_end(*kv_rows)
    ffn_far = second_step(ffn_near, kv_all)
    point_far = second_step(point_near, *ffn_far)
    bucket_window = lax.dynamic_slice_in_dim(
        jnp.pad(rel_bucket, (1, 0), constant_values=-1),
        full_len - bin_count - seq_pos * bin_count,
        full_len + bin_count,
    )
    window_onehot = (bucket_window[:, None] == jnp.arange(NB)[None, :]).astype(wide)
    distance_bias = lax.dot_general(
        table_flat.reshape(HEADS, NB), window_onehot, (((1,), (1,)), ((), ())),
        precision=lax.Precision.HIGHEST, preferred_element_type=wide,
    ).reshape(pairs, 2, full_len + bin_count)
    mixed = attn_fwd(query_rows, kv_all, distance_bias)
    second_sum = first_sum + dense(mixed, w_out)
    ffn_far = [tie(x, second_sum) for x in ffn_far]
    (w_up, w_down) = sorted_rows(
        parts(ffn_near, ffn_far),
        [
            (1, hidden, [(0, hidden, 0, 0)]),
            (2, chans, [(hidden, chans, 0, 0), (hidden + chans, chans, 1, 0)]),
        ],
    )
    normed_two = layer_norm(second_sum, gain_ffn, shift_ffn).astype(low)
    up_pre = dense(normed_two, w_up) + bias_up
    up_act, up_slope = gelu_and_slope(up_pre)
    third_sum = second_sum + dense(up_act, w_down) + bias_down
    third_rows = gather_begin(tie(third_sum.astype(low), w_head))
    point_far = [tie(x, third_rows[0]) for x in point_far]
    third_all = gather_end(*third_rows)
    (w_point,) = sorted_rows(
        parts(point_near, point_far),
        [(1, point_weight.shape[1], [(0, point_weight.shape[1], 0, 0)])],
    )
    crop_at = crop_start[0, 0]
    cropped = lax.dynamic_slice_in_dim(third_all, crop_at, crop_rows, 0)
    point_pre = dense(cropped, w_point) + bias_point
    point_act, point_slope = gelu_and_slope(point_pre)

    human_act = jnp.where(lower, point_act, to_upper_core(point_act))
    column = jnp.arange(BLOCK)
    first_valid = 3 * BLOCK * seq_pos + jnp.where(lower, 0, 2 * BLOCK) + column < tracks
    second_valid = jnp.where(
        lower, 3 * BLOCK * seq_pos + BLOCK + column < tracks, BLOCK * seq_pos + column < TRK_M
    )
    preds, logit_grads = [], []
    for which, act, valid in ((0, human_act, first_valid), (1, point_act, second_valid)):
        span = slice(which * BLOCK, (which + 1) * BLOCK)
        mask = valid.astype(wide)
        logits = dense(act, w_head[:, span])
        preds.append((jax.nn.softplus(logits) * mask).astype(low))
        logit_grads.append(
            (track_grad[:, span].astype(wide) * mask * jax.nn.sigmoid(logits)).astype(low)
        )
    arrived = to_lower_core(dense_back(logit_grads[0], w_head[:, :BLOCK]).astype(low))
    logit_grad = jnp.concatenate(logit_grads, axis=1)
    own_grad = jnp.concatenate(
        [jnp.where(lower, logit_grads[0], jnp.zeros_like(logit_grads[0])), logit_grads[1]], axis=1
    )
    point_act_grad = dense_back(own_grad, w_head) + jnp.where(lower, arrived.astype(wide), 0.0)

    point_grad = (point_slope.astype(wide) * point_act_grad).astype(low)
    crop_grad = dense_back(point_grad, w_point).astype(low)
    third_blocks = scatter_blocks(place_rows(crop_grad, crop_at, full_len))
    third_mine, third_onward = scatter_begin(*third_blocks)
    head_part = tracks_grad(human_act, point_act, tie(logit_grad, *third_blocks[0])).reshape(
        dp_count, -1, 2 * BLOCK
    )
    point_grad = tie(point_grad, *third_blocks[0])
    point_sent = outer_half(cropped, point_grad, 1)
    point_other = swap_cores(point_sent)
    third_onward = [tie(x, head_part, point_sent) for x in third_onward]
    head_sum = lax.psum_scatter(head_part, "dp", scatter_dimension=0, tiled=False)
    grad_point_b = row_sum(point_grad)
    point_half = by_device(outer_half(cropped, point_grad, 0, point_other))
    third_grad = tie(scatter_end(third_mine, third_onward), point_half)

    preds = exchange_plane(
        tie(jnp.concatenate(preds, axis=1), third_grad).reshape(4, crop_rows // 4, 2 * BLOCK)
    )
    down_grad = third_grad.astype(low)
    down_other = swap_cores(outer_half(up_act, down_grad, 1))
    grad_down_b = row_sum(down_grad)
    up_grad = (up_slope.astype(wide) * dense_back(down_grad, w_down)).astype(low)
    point_once = fold_both(point_half, 0, (down_other,))
    down_half = by_device(outer_half(up_act, down_grad, 0, down_other))
    up_grad = tie(up_grad, down_half)

    up_other = swap_cores(outer_half(normed_two, up_grad, 1))
    grad_up_b = row_sum(up_grad)
    _, norm_two_back = jax.vjp(layer_norm, second_sum, gain_ffn, shift_ffn)
    second_part, grad_ffn_gain, grad_ffn_shift = norm_two_back(dense_back(up_grad, w_up))
    second_grad = third_grad + second_part
    out_grad = second_grad.astype(low)
    mixed_grad = dense_back(out_grad, w_out).astype(low)
    up_half = by_device(outer_half(normed_two, up_grad, 0, up_other))
    mixed_grad = tie(mixed_grad, up_half, preds, *point_once)

    out_other = swap_cores(outer_half(mixed, out_grad, 1))
    query_low, kv_part, distance_grad = attn_bwd(
        query_rows, kv_all, distance_bias, mixed_grad
    )
    point_twice = fold_both(point_once, 1, (kv_part,))
    down_once = fold_both(down_half, 0, (kv_part,))
    kv_part = tie(kv_part, out_other, *point_twice, *down_once)

    kv_mine, kv_onward = scatter_begin(*scatter_blocks(kv_part))
    grad_table = jnp.dot(
        distance_grad.reshape(HEADS, -1), window_onehot, precision=lax.Precision.HIGHEST,
        preferred_element_type=wide,
    ).reshape(HEADS * NB)
    out_half = by_device(outer_half(mixed, out_grad, 0, out_other))
    kv_onward = [tie(x, out_half, head_sum) for x in kv_onward]
    kv_low = scatter_end(kv_mine, kv_onward).astype(low)

    mixer_grads = jnp.concatenate([kv_low, query_low], axis=1)
    mixer_sent = outer_half(normed_one, mixer_grads, 1)
    mixer_other = swap_cores(mixer_sent)
    down_twice = fold_both([tie(x, *kv_onward) for x in down_once], 1, (kv_low,))
    up_once = fold_both(tie(up_half, *kv_onward), 0, (mixer_sent,))
    normed_one_grad = dense_back(kv_low, w_kv) + dense_back(tie(query_low, mixer_sent), w_query)
    _, norm_one_back = jax.vjp(layer_norm, first_sum, gain_attn, shift_attn)
    first_part, grad_attn_gain, grad_attn_shift = norm_one_back(normed_one_grad)
    first_grad = second_grad + first_part
    conv_grad = first_grad.astype(low)
    grad_conv_b = row_sum(conv_grad)
    conv_part = exchange_plane(
        conv_grad.reshape(bin_count, 4, outputs).transpose(1, 0, 2)
    ).reshape(full_len, outputs)
    mixer_half = jnp.concatenate(
        [by_device(outer_half(normed_one, mixer_grads, 0, mixer_other)), out_half], axis=-1
    )
    up_twice = fold_both(up_once, 1, (conv_grad,))
    rest_sum = lax.psum_scatter(
        jnp.concatenate(
            [*point_twice, *up_twice]
            + [x[:, rows] for rows in (slice(0, depth), slice(depth, None)) for x in down_twice],
            axis=-1,
        ),
        "dp", scatter_dimension=0, tiled=False,
    ).astype(wide)
    conv_part = tie(conv_part, mixer_half, *up_twice)

    mixer_once = fold_both(mixer_half, 0)
    padded = jnp.pad(conv_part, ((half_width, half_width), (0, 0)))
    taps = jnp.concatenate(
        [padded[2 * half_width - k : 2 * half_width - k + full_len] for k in range(WIDTH)], axis=1
    )
    conv_sent = outer_half(act_all, taps, 1, taps=WIDTH)
    conv_other = swap_cores(conv_sent)
    act_part = conv_back(tie(taps, conv_sent), w_conv)
    conv_sum = outer_half(act_all, tie(taps, act_part), 0, conv_other, taps=WIDTH)
    act_part = tie(act_part, *mixer_once)
    mixer_twice = fold_both(mixer_once, 1)
    act_mine, act_onward = scatter_begin(*scatter_blocks(act_part))
    act_onward = [tie(x, *mixer_twice) for x in act_onward]
    act_grad = scatter_end(act_mine, act_onward)
    predictions = collect_tracks(tie(preds, *act_onward), tracks, low)
    grad_mixer = lax.psum_scatter(
        jnp.concatenate(mixer_twice, axis=-1), "dp", scatter_dimension=0, tiled=False
    ).astype(wide)
    conv_sum = lax.psum_scatter(
        conv_sum.reshape(dp_count, -1, outputs), "dp", scatter_dimension=0, tiled=False
    )
    grad_conv_w = exchange_plane(conv_sum.reshape(4, -1, outputs))
    grad_conv_w = grad_conv_w.transpose(1, 0, 2).reshape(-1, chans).astype(wide)
    head_grad = collect_tracks(
        exchange_plane(tie(head_sum, *act_onward).reshape(4, head_rows, 2 * BLOCK)), tracks, wide
    )
    grad_point_w = rest_sum[:, : point_weight.shape[1]]
    at = point_weight.shape[1]
    grad_up_w = rest_sum[:, at : at + hidden]
    at += hidden
    grad_down_w = jnp.concatenate([rest_sum[:, at : at + chans], rest_sum[:, at + chans :]], axis=0)
    normed_rows_gradient = act_slope.astype(wide) * act_grad
    vectors = (
        jnp.sum(normed_rows_gradient * standardized_input, axis=0),
        jnp.sum(normed_rows_gradient, axis=0),
        grad_table,
        grad_conv_b,
        grad_attn_gain,
        grad_attn_shift,
        grad_ffn_gain,
        grad_ffn_shift,
        grad_up_b,
        grad_down_b,
        grad_point_b,
    )
    summed = sum_column(sum_chips(jnp.concatenate(vectors).reshape(-1, 128))).reshape(-1)
    standardized_sum, plain_gradient_sum = summed[:chans], summed[chans : 2 * chans]
    input_grad = first_grad + batchnorm_gain * inverse_deviation * (
        normed_rows_gradient
        - plain_gradient_sum / element_count
        - standardized_input * standardized_sum / element_count
    )
    shares = []
    at = 0
    for x in vectors:
        size = x.shape[0] // device_count
        shares.append(lax.dynamic_slice_in_dim(summed, at + portion_index * size, size))
        at += x.shape[0]
    bn_gain_share, bn_shift_share, table_share, conv_b_share = shares[:4]
    attn_gain_share, attn_shift_share, ffn_gain_share, ffn_shift_share = shares[4:8]
    up_b_share, down_b_share, point_b_share = shares[8:]
    kv_share = grad_mixer[:, :kv_width].reshape(-1, pairs, PAIR)
    key_share = kv_share[:, :, : 2 * QK].reshape(-1, key_weight.shape[1])
    value_share = kv_share[:, :, 2 * QK :].reshape(-1, value_weight.shape[1])
    query_share = grad_mixer[:, kv_width : kv_width + q_width]
    out_share = grad_mixer[:, kv_width + q_width :]
    return (
        predictions[None, None],
        input_grad[None, None],
        grad_conv_w,
        query_share,
        key_share,
        value_share,
        out_share,
        grad_up_w,
        grad_down_w,
        grad_point_w,
        table_share,
        bn_gain_share,
        bn_shift_share,
        conv_b_share,
        attn_gain_share,
        attn_shift_share,
        ffn_gain_share,
        ffn_shift_share,
        up_b_share,
        down_b_share,
        point_b_share,
        head_grad[None],
    )


def solution(mesh):
    everywhere = P(EVERYWHERE)
    rows = P(EVERYWHERE, None)
    bins = P("species", "dp", "seq", None)
    head = P("species", ("dp", "seq"), None)
    return jax.shard_map(
        on_device,
        mesh=mesh,
        in_specs=(bins, P("species", "dp"), P()) + (rows,) * 8 + (everywhere,) * 11 + (head, bins),
        out_specs=(bins, bins) + (rows,) * 8 + (everywhere,) * 11 + (head,),
        check_vma=False,
    )
```
